256 devices in a mesh: tm: 4 (over x), space: 64 (over z, y, core).
Axes of the slice: x: 4, y: 4, z: 8, core: 2. Of those that a mesh axis runs over, the one named last changes fastest.
Arguments:
- flow_state: float32 [16, 6, 128, 32, 128], P('tm', None, 'space'), may hold values from -0.65 to 3.75, as said below
- metrics: float32 [11, 128, 32, 128], P(None, 'space', 'tm'), may hold values from -0.3 to 2, as said below
Outputs:
- increment: float32 [16, 6, 128, 32, 128], P('tm', None, 'space')
The draws below stay inside these ranges and needn't reach their ends.
Inputs may be any that keep to these rules, and one draw needn't show every extreme that they name: `flow_state`: physical conserved states: density between 0.7 and 1.3, speed components below 0.5 in magnitude, pressure between 0.7 and 1.3, turbulent viscosity between 0.01 and 0.1. `metrics`: face vectors have a leading component between 0.7 and 1.3 along their own dimension and others of at most 0.3; volumes lie between 0.6 and 1.6, wall distances between 0.2 and 2.
All inputs are finite; a program needn't handle non-finite values.
Results may differ from the reference program's by a relative error of at most 0.00023.
Values sent between devices are 32-bit elements; how exact they have to be, the bound alone decides.
A program may use at most 64 MiB of HBM per device.

```python
import math
import jax
import jax.numpy as jnp
import numpy as np
from jax import lax

NINST = 16
NMET = 11
SECTIONS = 2
CY = 32
CZ = 128
NX = 128


def draw_flow_state(key, part):
    key = jax.random.fold_in(key, 11)
    subkeys = jax.random.split(key, 4)
    shape_cell = (NINST, NX, CY, CZ)
    density = jax.random.uniform(subkeys[0], shape_cell, minval=0.7, maxval=1.3)
    speeds = jax.random.uniform(subkeys[1], (3,) + shape_cell, minval=-0.5, maxval=0.5)
    pressure = jax.random.uniform(subkeys[2], shape_cell, minval=0.7, maxval=1.3)
    turbulent = jnp.exp(jax.random.uniform(subkeys[3], shape_cell, minval=math.log(0.01), maxval=math.log(0.1)))
    momentum = density[None] * speeds
    energy = pressure / 0.4 + 0.5 * density * (speeds[0] * speeds[0] + speeds[1] * speeds[1] + speeds[2] * speeds[2])
    stacked = jnp.stack([density, momentum[0], momentum[1], momentum[2], energy, density * turbulent], axis=1)
    return stacked.astype(jnp.float32)


def draw_metrics(key, part):
    key = jax.random.fold_in(key, 23)
    uniform_raw = jax.random.uniform(key, (NMET, NX, CY, CZ))
    component = lax.broadcasted_iota(jnp.int32, (NMET, 1, 1, 1), 0)
    leading = (component < 9) & (component // 3 == component % 3)
    face_values = jnp.where(leading, 0.7 + 0.6 * uniform_raw, -0.3 + 0.6 * uniform_raw)
    volume = jnp.exp(math.log(0.6) + uniform_raw * math.log(1.6 / 0.6))
    distance = jnp.exp(math.log(0.2) + uniform_raw * math.log(10.0))
    values = jnp.where(component < 9, face_values, jnp.where(component == 9, volume, distance))
    return values.astype(jnp.float32)


def setup_inputs(seed: int = 0) -> dict:
    key_of = jax.random.split(jax.random.key(seed), 3)
    flow_state = draw_flow_state(jax.random.fold_in(key_of[2], 71), 0)
    metrics = draw_metrics(jax.random.fold_in(key_of[2], 71), 0)
    return dict(flow_state=flow_state, metrics=metrics)


GAMMA = 1.4
EPS_TWO = 0.1
EPS_FOUR = 0.03125
VISCOSITY = 0.02
HEAT_FACTOR = 1.4 / (0.4 * 0.72)
TURB_DIFFUSE = 1.5
WALL_COEFF = 3.24
OMEGA = 1.0
CFL_NUMBER = 0.5

def spectral_table(length):
    table_rows = []
    for first in range(length):
        entries = []
        for second in range(length):
            offset = first - second
            if offset == 0:
                entries.append(0.0)
            else:
                parity = 1.0 if offset % 2 == 0 else -1.0
                entries.append(0.5 * parity / math.tan(math.pi * offset / length))
        table_rows.append(entries)
    return np.array(table_rows)

def primitives(states):
    density = states[:, 0]
    velocity = states[:, 1:4] / density[:, None]
    pressure = (GAMMA - 1.0) * (states[:, 4] - 0.5 * lax.optimization_barrier(jnp.sum(states[:, 1:4] * velocity, axis=1)))
    return (density, velocity, pressure)

def convective(states, velocity, pressure, normal):
    normal_flow = lax.optimization_barrier(jnp.sum(velocity * normal[None], axis=1))
    mass_flux = states[:, 0] * normal_flow
    momentum_flux = states[:, 1:4] * normal_flow[:, None] + pressure[:, None] * normal[None]
    energy_flux = (states[:, 4] + pressure) * normal_flow
    turbulent_flux = states[:, 5] * normal_flow
    return jnp.concatenate([mass_flux[:, None], momentum_flux, energy_flux[:, None], turbulent_flux[:, None]], axis=1)

def spectral_radius(left_cells, right_cells, normal):
    left_rho, left_vel, left_pre = primitives(left_cells)
    right_rho, right_vel, right_pre = primitives(right_cells)
    normal_flow = 0.5 * lax.optimization_barrier(jnp.sum((left_vel + right_vel) * normal[None], axis=1))
    sound_speed = 0.5 * (jnp.sqrt(GAMMA * left_pre / left_rho) + jnp.sqrt(GAMMA * right_pre / right_rho))
    return jnp.abs(normal_flow) + sound_speed * jnp.sqrt(lax.optimization_barrier(jnp.sum(normal * normal, axis=0)))[None]

def face_flux(outer_left, left_cells, right_cells, outer_right, normal, left_volume, right_volume, radius):
    left_rho, left_vel, left_pre = primitives(left_cells)
    right_rho, right_vel, right_pre = primitives(right_cells)
    central = 0.5 * (convective(left_cells, left_vel, left_pre, normal) + convective(right_cells, right_vel, right_pre, normal))
    jump_one = right_cells - left_cells
    jump_three = outer_right - 3.0 * right_cells + 3.0 * left_cells - outer_left
    damping = radius[:, None] * (EPS_TWO * jump_one - EPS_FOUR * jump_three)
    mu_face = VISCOSITY + 0.5 * (left_cells[:, 5] + right_cells[:, 5])
    conduct = mu_face * (lax.optimization_barrier(jnp.sum(normal * normal, axis=0)) / (0.5 * (left_volume + right_volume)))[None]
    kinetic_jump = 0.5 * (lax.optimization_barrier(jnp.sum(right_vel * right_vel, axis=1)) - lax.optimization_barrier(jnp.sum(left_vel * left_vel, axis=1)))
    heat_jump = HEAT_FACTOR * (right_pre / right_rho - left_pre / left_rho)
    turb_jump = TURB_DIFFUSE * (right_cells[:, 5] / right_rho - left_cells[:, 5] / left_rho)
    viscous = jnp.concatenate([jnp.zeros_like(kinetic_jump)[:, None], right_vel - left_vel, (kinetic_jump + heat_jump)[:, None], turb_jump[:, None]], axis=1)
    return central - damping - conduct[:, None] * viscous

def source_terms(states, distance, volume):
    destroy = WALL_COEFF * volume[None] * states[:, 5] * states[:, 5] / (states[:, 0] * (distance * distance)[None])
    blank_terms = jnp.zeros(states.shape[:1] + (5,) + states.shape[2:], jnp.float32)
    return jnp.concatenate([blank_terms, destroy[:, None]], axis=1)

def radii_and_step(states, metrics):
    volume = metrics[9]
    radius_list = []
    denominator = OMEGA * 0.5 * NINST * volume[None]
    for direction in range(3):
        radius = spectral_radius(states, jnp.roll(states, -1, direction + 2), metrics[3 * direction:3 * direction + 3])
        radius_list.append(radius)
        denominator = denominator + radius + jnp.roll(radius, 1, direction + 1)
    return (jnp.stack(radius_list), CFL_NUMBER / denominator)

def flux_residual(states, metrics, face_radii):
    volume = metrics[9]
    summed = source_terms(states, metrics[10], volume)
    for direction in range(3):
        axis_state = direction + 2
        face_terms = face_flux(jnp.roll(states, 1, axis_state), states, jnp.roll(states, -1, axis_state), jnp.roll(states, -2, axis_state), metrics[3 * direction:3 * direction + 3], volume, jnp.roll(volume, -1, direction), face_radii[direction])
        summed = summed + face_terms - jnp.roll(face_terms, 1, axis_state)
    return summed

def reference(flow_state, metrics):
    time_table = jnp.asarray(spectral_table(NINST)).astype(jnp.float32)
    volume = metrics[9]
    face_radii, pseudo_step = lax.map(lambda single: radii_and_step(single[None], metrics), flow_state)
    face_radii = face_radii[:, :, 0]
    pseudo_step = pseudo_step[:, 0]
    current = flow_state
    for section_index in range(SECTIONS):
        coupled = jnp.dot(time_table, current.reshape(NINST, -1), precision=lax.Precision.HIGHEST).reshape(current.shape)

        def one_instance(operands):
            single, radius_set, coupling = operands
            spatial = flux_residual(single[None], metrics, radius_set[:, None])[0]
            return spatial + OMEGA * volume[None] * coupling
        residual = lax.map(one_instance, (current, face_radii, coupled))
        current = flow_state - 1.0 / (SECTIONS - section_index) * pseudo_step[:, None] * residual
    return current - flow_state
```

```python
import math

import jax
import jax.numpy as jnp
from jax import lax
from jax.experimental import pallas as pl
from jax.experimental.pallas import tpu as pltpu
from jax.sharding import PartitionSpec as P

NINST = 16
GROUPS = 4
PER = 4
TILES = 12
GAMMA = 1.4
EPS_TWO = 0.1
EPS_FOUR = 0.03125
JUMP_RATIO = (EPS_TWO + 3.0 * EPS_FOUR) / EPS_FOUR
VISCOSITY = 0.02
HEAT_FACTOR = 1.4 / (0.4 * 0.72)
TURB_DIFFUSE = 1.5
WALL_COEFF = 3.24
MESH = pl.DeviceIdType.MESH


def table_entry(offset):
    offset = offset % NINST
    if offset == 0 or offset == NINST // 2:
        return 0.0
    parity = 1.0 if offset % 2 == 0 else -1.0
    return 0.5 * parity / math.tan(math.pi * offset / NINST)


def lane_roll(x, k):
    k = k % 128
    return x if k == 0 else pltpu.roll(x, k, 1)


def row_roll(x, k):
    k = k % 8
    return x if k == 0 else pltpu.roll(x, k, 0)


class Masks:
    def __init__(self):
        lane = lax.broadcasted_iota(jnp.int32, (8, 128), 1)
        self.row = lax.broadcasted_iota(jnp.int32, (8, 128), 0)
        self.zlo = lane & 31
        self.half = lane < 64
        self.even = (lane & 32) == 0


def swap_segments(m, x):
    a0 = jnp.where(m.half, x[0], lane_roll(x[2], 64))
    a2 = jnp.where(m.half, lane_roll(x[0], 64), x[2])
    a1 = jnp.where(m.half, x[1], lane_roll(x[3], 64))
    a3 = jnp.where(m.half, lane_roll(x[1], 64), x[3])
    return [
        jnp.where(m.even, a0, lane_roll(a1, 32)),
        jnp.where(m.even, lane_roll(a0, -32), a1),
        jnp.where(m.even, a2, lane_roll(a3, 32)),
        jnp.where(m.even, lane_roll(a2, -32), a3),
    ]


def pack_edge(m, acc, tile, k, first):
    moved = lane_roll(tile, 2 * k - first)
    return moved if acc is None else jnp.where((m.zlo >> 1) == k, moved, acc)


def y_up(m, w, w32, k):
    return row_roll(jnp.where(m.row < k, w32, w), -k)


def y_down(m, w, k):
    return row_roll(jnp.where(m.row >= 8 - k, lane_roll(w, 32), w), k)


def primitives(w):
    inv = 1.0 / w[0]
    u = [w[1] * inv, w[2] * inv, w[3] * inv]
    kin = 0.5 * (w[1] * u[0] + w[2] * u[1] + w[3] * u[2])
    p = (GAMMA - 1.0) * (w[4] - kin)
    temp = p * inv
    return dict(
        u=u,
        p=p,
        h=w[4] + p,
        e=kin * inv + HEAT_FACTOR * temp,
        n=TURB_DIFFUSE * (w[5] * inv),
        t=temp,
    )


def half_sound(prim):
    return 0.5 * jnp.sqrt(GAMMA * prim["t"])


def dot3(a, b):
    return a[0] * b[0] + a[1] * b[1] + a[2] * b[2]


def face(wm, wl, wr, wp, pl_, pr_, geo, scaled=None):
    hs, length, cond = geo[0:3], geo[3], geo[4]
    ql = dot3(pl_["u"], hs)
    qr = dot3(pr_["u"], hs)
    rad = None
    if scaled is None:
        rad = jnp.abs(ql + qr) + (half_sound(pl_) + half_sound(pr_)) * length
        scaled = EPS_FOUR * rad
    g = (VISCOSITY + 0.5 * (wl[5] + wr[5])) * cond
    psum = pl_["p"] + pr_["p"]
    out = []
    for f in range(6):
        if f == 4:
            c = pl_["h"] * ql + pr_["h"] * qr
        else:
            c = wl[f] * ql + wr[f] * qr
        if 1 <= f <= 3:
            c = c + psum * hs[f - 1] - g * (pr_["u"][f - 1] - pl_["u"][f - 1])
        if f == 4:
            c = c - g * (pr_["e"] - pl_["e"])
        if f == 5:
            c = c - g * (pr_["n"] - pl_["n"])
        d = wr[f] - wl[f]
        out.append(c - scaled * (JUMP_RATIO * d - (wp[f] - wm[f])))
    return out, rad, scaled


def geometry(s, left_volume, right_volume):
    sq = dot3(s, s)
    return [0.5 * s[0], 0.5 * s[1], 0.5 * s[2], jnp.sqrt(sq), sq / (0.5 * (left_volume + right_volume))]


def geometry_known(s, cond):
    return [0.5 * s[0], 0.5 * s[1], 0.5 * s[2], jnp.sqrt(dot3(s, s)), cond]


def kernel(
    flow, metrics, out,
    xv, mv, sbuf, region, hl0, hr0, res, w1, zs, z1, hl1, hr1, ob, oin, ov,
    ms, mr, mt, mleft, mright, gx, gy, gz, ry, rz, rx, den, step,
    in_sem, own_sem, out_sem, met_s, met_r, pm_s, pm_r,
    xin_s, xin_r, fw_s, fw_r, wp_s, wp_r, z_s, z_r, o_s, o_r,
):
    t = lax.axis_index("tm")
    s = lax.axis_index("space")
    nt = lax.axis_size("tm")
    ns = lax.axis_size("space")
    right = (t, lax.rem(s + 1, ns))
    left = (t, lax.rem(s + ns - 1, ns))

    def group(k):
        return lax.rem(t + k, nt)

    def remote(src, dst, ss, rs, dev):
        return pltpu.make_async_remote_copy(
            src_ref=src, dst_ref=dst, send_sem=ss, recv_sem=rs, device_id=dev, device_id_type=MESH
        )

    barrier = pltpu.get_barrier_semaphore()
    for dev in ((group(1), s), (group(2), s), (group(3), s), left, right):
        pl.semaphore_signal(barrier, inc=1, device_id=dev, device_id_type=MESH)

    load_m = pltpu.make_async_copy(metrics, mv, in_sem.at[PER])
    load_m.start()

    def load_x(j):
        return pltpu.make_async_copy(flow.at[j], xv.at[j], in_sem.at[j])

    for j in range(PER):
        load_x(j).start()

    m = Masks()
    load_m.wait()
    for quad in range(8):
        tiles = []
        for e in range(4 * quad, 4 * quad + 4):
            p, e = divmod(e, 16)
            sz = [mv[6 + c, p] for c in range(3)]
            vol = mv[9, p]
            if e < 3:
                tiles.append(mv[e, p])
            elif e == 3:
                tiles.append(vol)
            elif e < 7:
                tiles.append(mv[e - 1, p])
            elif e < 10:
                tiles.append(sz[e - 7])
            elif e < 13:
                tiles.append(lane_roll(sz[e - 10], 1))
            elif e < 15:
                cond = dot3(sz, sz) / (0.5 * (vol + lane_roll(vol, -1)))
                tiles.append(cond if e == 13 else lane_roll(cond, 1))
            else:
                tiles.append(WALL_COEFF * vol / (mv[10, p] * mv[10, p]))
        for b, tile in enumerate(swap_segments(m, tiles)):
            ms[b, quad] = tile

    def pack(j):
        load_x(j).wait()
        low = [None] * 4
        high = [None] * 4
        for q in range(TILES):
            f, p = divmod(q, 2)
            tiles = swap_segments(m, [xv[j, f, p, 8 * y : 8 * y + 8, :] for y in range(4)])
            for b in range(4):
                sbuf[b, j, q] = tiles[b]
                low[b] = pack_edge(m, low[b], tiles[b], q, 0)
                high[b] = pack_edge(m, high[b], tiles[b], q, 30)
        for b in range(4):
            sbuf[(b + 1) % 4, j, TILES] = high[b]
            sbuf[(b + 3) % 4, j, TILES + 1] = low[b]

    def met_copy(k):
        return remote(ms.at[group(k)], mr.at[t], met_s.at[k - 1], met_r.at[k - 1], (group(k), s))

    def met_arrival(k):
        return remote(ms.at[t], mr.at[group(4 - k)], met_s.at[k - 1], met_r.at[k - 1], (group(k), s))

    def xin_copy(k, j):
        return remote(
            sbuf.at[group(k), j], region.at[t * PER + j],
            xin_s.at[k - 1, j], xin_r.at[k - 1, j], (group(k), s),
        )

    def xin_arrival(k, j):
        return remote(
            sbuf.at[t, j], region.at[group(4 - k) * PER + j],
            xin_s.at[k - 1, j], xin_r.at[k - 1, j], (group(k), s),
        )

    def forward(src, i):
        return (
            remote(src, hl0.at[i], fw_s.at[0, i], fw_r.at[0, i], right),
            remote(src, hr0.at[i], fw_s.at[1, i], fw_r.at[1, i], left),
        )

    def own_copy(j):
        return pltpu.make_async_copy(sbuf.at[t, j], region.at[t * PER + j], own_sem.at[j])

    mr[t] = ms[t]
    pl.semaphore_wait(barrier, 5)
    for k in (2, 1, 3):
        met_copy(k).start()

    @pl.loop(0, PER)
    def _(j):
        pack(j)
        for k in (2, 1, 3):
            xin_copy(k, j).start()
        for c in forward(sbuf.at[t, j, pl.ds(0, TILES)], t * PER + j):
            c.start()
        own_copy(j).start()

    for k in (2, 1, 3):
        met_arrival(k).wait_recv()
    for quad in range(8):
        for e, tile in enumerate(swap_segments(m, [mr[b, quad] for b in range(4)])):
            mt[4 * quad + e] = tile
    plane_metrics = (
        remote(mt.at[pl.ds(16, 4)], mleft, pm_s.at[0], pm_r.at[0], right),
        remote(mt.at[pl.ds(3, 1)], mright, pm_s.at[1], pm_r.at[1], left),
    )
    for c in plane_metrics:
        c.start()
    for p in range(2):
        o = 16 * p
        vol = mt[o + 3]
        sy = [mt[o + 4 + c] for c in range(3)]
        geo_y = geometry(sy, vol, y_up(m, vol, lane_roll(vol, -32), 1))
        geo_z = geometry_known([mt[o + 7 + c] for c in range(3)], mt[o + 13])
        geo_l = geometry_known([mt[o + 10 + c] for c in range(3)], mt[o + 14])
        for c in range(5):
            gy[p, c] = geo_y[c]
            gz[p, 0, c] = geo_z[c]
            gz[p, 1, c] = geo_l[c]

    def cross(i, w_of, low_pack, high_pack, first):
        for p in range(2):
            w = [w_of(f, p) for f in range(6)]
            prim = primitives(w)
            yu, yuu, yd, zu, zuu, zd, zdd = [], [], [], [], [], [], []
            for f in range(6):
                k = 2 * f + p
                w32 = lane_roll(w[f], -32)
                yu.append(y_up(m, w[f], w32, 1))
                yuu.append(y_up(m, w[f], w32, 2))
                yd.append(y_down(m, w[f], 1))
                hi = lane_roll(high_pack, 32 - 2 * k)
                lo = lane_roll(low_pack, -2 - 2 * k)
                zu.append(lane_roll(jnp.where(m.zlo == 0, hi, w[f]), -1))
                zuu.append(lane_roll(jnp.where(m.zlo < 2, hi, w[f]), -2))
                zd.append(lane_roll(jnp.where(m.zlo == 31, lo, w[f]), 1))
                zdd.append(lane_roll(jnp.where(m.zlo >= 30, lo, w[f]), 2))
            geo_y = [gy[p, c] for c in range(5)]
            geo_z = [gz[p, 0, c] for c in range(5)]
            geo_l = [gz[p, 1, c] for c in range(5)]
            known = (None, None, None) if first else (ry[i, p], rz[i, p, 0], rz[i, p, 1])
            fy, rad_y, sc_y = face(yd, w, yu, yuu, prim, primitives(yu), geo_y, known[0])
            fz, rad_z, sc_z = face(zd, w, zu, zuu, prim, primitives(zu), geo_z, known[1])
            fl, rad_l, sc_l = face(zdd, zd, w, zu, primitives(zd), prim, geo_l, known[2])
            if first:
                ry[i, p] = sc_y
                rz[i, p, 0] = sc_z
                rz[i, p, 1] = sc_l
                den[i, p] = rad_y + y_down(m, rad_y, 1) + rad_z + rad_l + 8.0 * mt[16 * p + 3]
            for f in range(6):
                r = fy[f] - y_down(m, fy[f], 1) + fz[f] - fl[f]
                if f == 5:
                    r = r + mt[16 * p + 15] * w[5] * w[5] / w[0]
                if not first:
                    r = r + res[i, 2 * f + p]
                res[i, 2 * f + p] = r

    def mix(w_of, first):
        pc = [0.5 * (table_entry(d) + table_entry(d - 8)) for d in range(5)]
        qc = [0.5 * (table_entry(d) - table_entry(d - 8)) for d in range(5)]

        @pl.loop(0, TILES)
        def _(q):
            vol = mt[lax.rem(q, 2) * 16 + 3]
            w = [w_of(i, q) for i in range(NINST)]
            b = [w[i] + w[i + 8] for i in range(8)]
            a = [w[i] - w[i + 8] for i in range(8)]
            a = a + [-x for x in a]
            for r in range(8):
                even = None
                odd = qc[4] * a[(r - 4) % 16]
                for d in range(1, 4):
                    e = pc[d] * (b[(r - d) % 8] - b[(r + d) % 8])
                    even = e if even is None else even + e
                    odd = odd + qc[d] * (a[(r - d) % 16] - a[(r + d) % 16])
                for i, v in ((r, even + odd), (r + 8, even - odd)):
                    v = vol * v
                    res[i, q] = res[i, q] + v if first else v

    def axial(i, w_of, hl, hr, first):
        planes = [
            [hl[i, 2 * f] for f in range(6)],
            [hl[i, 2 * f + 1] for f in range(6)],
            [w_of(f, 0) for f in range(6)],
            [w_of(f, 1) for f in range(6)],
            [hr[i, 2 * f] for f in range(6)],
            [hr[i, 2 * f + 1] for f in range(6)],
        ]
        prims = [primitives(w) for w in planes[1:5]]
        fluxes, radii = [], []
        for k in range(3):
            geo = [gx[k, c] for c in range(5)]
            fx, rad, sc = face(
                planes[k], planes[k + 1], planes[k + 2], planes[k + 3],
                prims[k], prims[k + 1], geo, None if first else rx[i, k],
            )
            if first:
                rx[i, k] = sc
            fluxes.append(fx)
            radii.append(rad)
        result = []
        for p in range(2):
            if first:
                h = 0.5 / (den[i, p] + radii[p] + radii[p + 1])
                step[i, p] = h
            else:
                h = step[i, p]
            result.append([h * (res[i, 2 * f + p] + (fluxes[p + 1][f] - fluxes[p][f])) for f in range(6)])
        return result

    @pl.loop(0, NINST)
    def _(n):
        own = n < PER
        far = jnp.maximum(n - PER, 0)
        j = jnp.where(own, n, far // 3)
        back = jnp.where(own, 0, lax.rem(far, 3) + 1)
        i = lax.rem(t + nt - back, nt) * PER + j

        @pl.when(own)
        def _():
            own_copy(j).wait()

        @pl.when(n >= PER)
        def _():
            xin_arrival(back, j).wait_recv()
            for c in forward(region.at[i, pl.ds(0, TILES)], i):
                c.start()

        cross(i, lambda f, p: region[i, 2 * f + p], region[i, TILES], region[i, TILES + 1], True)

    mix(lambda i, q: region[i, q], True)

    for c in plane_metrics:
        c.wait_recv()
    sx = [[mleft[c] for c in range(3)], [mt[c] for c in range(3)], [mt[16 + c] for c in range(3)]]
    vx = [mleft[3], mt[3], mt[19], mright[0]]
    for k in range(3):
        for c, g in enumerate(geometry(sx[k], vx[k], vx[k + 1])):
            gx[k, c] = g

    def order(n):
        return group(lax.rem(n, 4)) * PER + n // 4

    def edge_copies(i):
        return (
            remote(w1.at[i], hl1.at[i], wp_s.at[0, i], wp_r.at[0, i], right),
            remote(w1.at[i], hr1.at[i], wp_s.at[1, i], wp_r.at[1, i], left),
            remote(zs.at[i, 0], z1.at[i, 1], z_s.at[0, i], z_r.at[0, i], (group(3), s)),
            remote(zs.at[i, 1], z1.at[i, 0], z_s.at[1, i], z_r.at[1, i], (group(1), s)),
        )

    @pl.loop(0, NINST)
    def _(n):
        i = order(n)
        for c in forward(region.at[i, pl.ds(0, TILES)], i):
            c.wait_recv()
        change = axial(i, lambda f, p: region[i, 2 * f + p], hl0, hr0, True)
        low = high = None
        for q in range(TILES):
            f, p = divmod(q, 2)
            v = region[i, q] - 0.5 * change[p][f]
            w1[i, q] = v
            low = pack_edge(m, low, v, q, 0)
            high = pack_edge(m, high, v, q, 30)
        zs[i, 0] = low
        zs[i, 1] = high
        for c in edge_copies(i):
            c.start()

    mix(lambda i, q: w1[i, q], False)

    @pl.loop(0, NINST)
    def _(n):
        i = order(n)
        for c in edge_copies(i)[2:]:
            c.wait_recv()
        cross(i, lambda f, p: w1[i, 2 * f + p], z1[i, 0], z1[i, 1], False)

    def out_copy(k, j):
        g = group(k)
        return remote(
            ob.at[g * PER + j], oin.at[t, j], o_s.at[k - 1, j], o_r.at[k - 1, j], (g, s)
        )

    def out_arrival(k, j):
        return remote(
            ob.at[t * PER + j], oin.at[group(4 - k), j],
            o_s.at[k - 1, j], o_r.at[k - 1, j], (group(k), s),
        )

    def store_out(j):
        return pltpu.make_async_copy(ov.at[j], out.at[j], out_sem.at[j])

    @pl.loop(0, PER)
    def _(j):
        @pl.loop(0, 4)
        def _(k):
            g = group(k)
            i = g * PER + j
            for c in edge_copies(i)[:2]:
                c.wait_recv()
            change = axial(i, lambda f, p: w1[i, 2 * f + p], hl1, hr1, False)
            for q in range(TILES):
                f, p = divmod(q, 2)
                ob[i, q] = -change[p][f]

            @pl.when(k > 0)
            def _():
                out_copy(k, j).start()

            @pl.when(k == 0)
            def _():
                for q in range(TILES):
                    oin[t, j, q] = ob[i, q]

    @pl.loop(0, PER)
    def _(j):
        for k in range(1, 4):
            out_arrival(k, j).wait_recv()
        for q in range(TILES):
            f, p = divmod(q, 2)
            tiles = swap_segments(m, [oin[b, j, q] for b in range(4)])
            for y in range(4):
                ov[j, f, p, 8 * y : 8 * y + 8, :] = tiles[y]
        store_out(j).start()

    for k in (1, 2, 3):
        met_copy(k).wait_send()
    for c in plane_metrics:
        c.wait_send()

    @pl.loop(0, PER)
    def _(j):
        for k in (1, 2, 3):
            xin_copy(k, j).wait_send()
            out_copy(k, j).wait_send()

    @pl.loop(0, NINST)
    def _(i):
        for c in forward(region.at[i, pl.ds(0, TILES)], i):
            c.wait_send()
        for c in edge_copies(i):
            c.wait_send()

    for j in range(PER):
        store_out(j).wait()


def per_device(flow_state, metrics):
    tile = (8, 128)
    f32 = jnp.float32

    def vmem(*lead):
        return pltpu.VMEM(lead + tile, f32)

    dma = pltpu.SemaphoreType.DMA
    full = (NINST, TILES)
    return pl.pallas_call(
        kernel,
        out_shape=jax.ShapeDtypeStruct(flow_state.shape, f32),
        in_specs=[pl.BlockSpec(memory_space=pl.ANY)] * 2,
        out_specs=pl.BlockSpec(memory_space=pl.ANY),
        scratch_shapes=[
            pltpu.VMEM(flow_state.shape, f32),
            pltpu.VMEM(metrics.shape, f32),
            vmem(GROUPS, PER, TILES + 2),
            vmem(NINST, TILES + 2),
            vmem(*full),
            vmem(*full),
            vmem(*full),
            vmem(*full),
            vmem(NINST, 2),
            vmem(NINST, 2),
            vmem(*full),
            vmem(*full),
            vmem(*full),
            vmem(GROUPS, PER, TILES),
            pltpu.VMEM(flow_state.shape, f32),
            vmem(4, 8),
            vmem(4, 8),
            vmem(32),
            vmem(4),
            vmem(1),
            vmem(3, 5),
            vmem(2, 5),
            vmem(2, 2, 5),
            vmem(NINST, 2),
            vmem(NINST, 2, 2),
            vmem(NINST, 3),
            vmem(NINST, 2),
            vmem(NINST, 2),
            dma((PER + 1,)),
            dma((PER,)),
            dma((PER,)),
            dma((3,)),
            dma((3,)),
            dma((2,)),
            dma((2,)),
            dma((3, PER)),
            dma((3, PER)),
            dma((2, NINST)),
            dma((2, NINST)),
            dma((2, NINST)),
            dma((2, NINST)),
            dma((2, NINST)),
            dma((2, NINST)),
            dma((3, PER)),
            dma((3, PER)),
        ],
        compiler_params=pltpu.CompilerParams(
            collective_id=0, has_side_effects=True, vmem_limit_bytes=32 << 20
        ),
        cost_estimate=pl.CostEstimate(
            flops=100_000_000, bytes_accessed=1_800_000, transcendentals=200_000
        ),
        name="balance",
    )(flow_state, metrics)


def solution(mesh):
    return jax.shard_map(
        per_device,
        mesh=mesh,
        in_specs=(P("tm", None, "space", None, None), P(None, "space", "tm", None)),
        out_specs=P("tm", None, "space", None, None),
        check_vma=False,
    )
```

```python
import math

import jax
import jax.numpy as jnp
from jax import lax
from jax.experimental import pallas as pl
from jax.experimental.pallas import tpu as pltpu
from jax.sharding import PartitionSpec as P

NINST = 16
GROUPS = 4
PER = 4
TILES = 12
LAG = 6
GAMMA = 1.4
EPS_TWO = 0.1
EPS_FOUR = 0.03125
JUMP_RATIO = (EPS_TWO + 3.0 * EPS_FOUR) / EPS_FOUR
VISCOSITY = 0.02
HEAT_FACTOR = 1.4 / (0.4 * 0.72)
TURB_DIFFUSE = 1.5
WALL_COEFF = 3.24
MESH = pl.DeviceIdType.MESH


def table_entry(offset):
    offset = offset % NINST
    if offset == 0 or offset == NINST // 2:
        return 0.0
    parity = 1.0 if offset % 2 == 0 else -1.0
    return 0.5 * parity / math.tan(math.pi * offset / NINST)


def lane_roll(x, k):
    k = k % 128
    return x if k == 0 else pltpu.roll(x, k, 1)


def row_roll(x, k):
    k = k % 8
    return x if k == 0 else pltpu.roll(x, k, 0)


class Masks:
    def __init__(self):
        lane = lax.broadcasted_iota(jnp.int32, (8, 128), 1)
        self.row = lax.broadcasted_iota(jnp.int32, (8, 128), 0)
        self.zlo = lane & 31
        self.half = lane < 64
        self.even = (lane & 32) == 0


def swap_segments(m, x):
    a0 = jnp.where(m.half, x[0], lane_roll(x[2], 64))
    a2 = jnp.where(m.half, lane_roll(x[0], 64), x[2])
    a1 = jnp.where(m.half, x[1], lane_roll(x[3], 64))
    a3 = jnp.where(m.half, lane_roll(x[1], 64), x[3])
    return [
        jnp.where(m.even, a0, lane_roll(a1, 32)),
        jnp.where(m.even, lane_roll(a0, -32), a1),
        jnp.where(m.even, a2, lane_roll(a3, 32)),
        jnp.where(m.even, lane_roll(a2, -32), a3),
    ]


def pack_edge(m, acc, tile, k, first):
    moved = lane_roll(tile, 2 * k - first)
    return moved if acc is None else jnp.where((m.zlo >> 1) == k, moved, acc)


def y_up(m, w, w32, k):
    return row_roll(jnp.where(m.row < k, w32, w), -k)


def y_down(m, w, k):
    return row_roll(jnp.where(m.row >= 8 - k, lane_roll(w, 32), w), k)


def primitives(w):
    inv = 1.0 / w[0]
    u = [w[1] * inv, w[2] * inv, w[3] * inv]
    kin = 0.5 * (w[1] * u[0] + w[2] * u[1] + w[3] * u[2])
    p = (GAMMA - 1.0) * (w[4] - kin)
    temp = p * inv
    return dict(
        u=u,
        p=p,
        h=w[4] + p,
        e=kin * inv + HEAT_FACTOR * temp,
        n=TURB_DIFFUSE * (w[5] * inv),
        t=temp,
    )


def half_sound(prim):
    return 0.5 * jnp.sqrt(GAMMA * prim["t"])


def dot3(a, b):
    return a[0] * b[0] + a[1] * b[1] + a[2] * b[2]


def face(wl, wr, outer, pl_, pr_, geo, scaled=None):
    hs, length, cond = geo[0:3], geo[3], geo[4]
    ql = dot3(pl_["u"], hs)
    qr = dot3(pr_["u"], hs)
    rad = None
    if scaled is None:
        rad = jnp.abs(ql + qr) + (half_sound(pl_) + half_sound(pr_)) * length
        scaled = EPS_FOUR * rad
    g = (VISCOSITY + 0.5 * (wl[5] + wr[5])) * cond
    psum = pl_["p"] + pr_["p"]
    out = []
    for f in range(6):
        if f == 4:
            c = pl_["h"] * ql + pr_["h"] * qr
        else:
            c = wl[f] * ql + wr[f] * qr
        if 1 <= f <= 3:
            c = c + psum * hs[f - 1] - g * (pr_["u"][f - 1] - pl_["u"][f - 1])
        if f == 4:
            c = c - g * (pr_["e"] - pl_["e"])
        if f == 5:
            c = c - g * (pr_["n"] - pl_["n"])
        d = wr[f] - wl[f]
        out.append(c - scaled * (JUMP_RATIO * d - outer(f)))
    return out, rad, scaled


def geometry(s, left_volume, right_volume):
    sq = dot3(s, s)
    return [0.5 * s[0], 0.5 * s[1], 0.5 * s[2], jnp.sqrt(sq), sq / (0.5 * (left_volume + right_volume))]


def geometry_known(s, cond):
    return [0.5 * s[0], 0.5 * s[1], 0.5 * s[2], jnp.sqrt(dot3(s, s)), cond]


def kernel(
    flow, metrics, out,
    xv, mv, sbuf, region, hl0, hr0, res, w1, zs, z1, hl1, hr1, ob, oin, ov,
    ms, mr, mt, mleft, mright, gx, gy, gz, ry, rz, rx, den, step,
    in_sem, own_sem, out_sem, met_s, met_r, pm_s, pm_r,
    xin_s, xin_r, fw_s, fw_r, wp_s, wp_r, z_s, z_r, o_s, o_r,
):
    t = lax.axis_index("tm")
    s = lax.axis_index("space")
    nt = lax.axis_size("tm")
    ns = lax.axis_size("space")
    right = (t, lax.rem(s + 1, ns))
    left = (t, lax.rem(s + ns - 1, ns))

    def group(k):
        return lax.rem(t + k, nt)

    def remote(src, dst, ss, rs, dev):
        return pltpu.make_async_remote_copy(
            src_ref=src, dst_ref=dst, send_sem=ss, recv_sem=rs, device_id=dev, device_id_type=MESH
        )

    barrier = pltpu.get_barrier_semaphore()
    for dev in ((group(1), s), (group(2), s), (group(3), s), left, right):
        pl.semaphore_signal(barrier, inc=1, device_id=dev, device_id_type=MESH)

    load_m = pltpu.make_async_copy(metrics, mv, in_sem.at[PER])
    load_m.start()

    def load_x(j):
        return pltpu.make_async_copy(flow.at[j], xv.at[j], in_sem.at[j])

    for j in range(PER):
        load_x(j).start()

    m = Masks()
    load_m.wait()
    for quad in range(8):
        tiles = []
        for e in range(4 * quad, 4 * quad + 4):
            p, e = divmod(e, 16)
            sz = [mv[6 + c, p] for c in range(3)]
            vol = mv[9, p]
            if e < 3:
                tiles.append(mv[e, p])
            elif e == 3:
                tiles.append(vol)
            elif e < 7:
                tiles.append(mv[e - 1, p])
            elif e < 10:
                tiles.append(sz[e - 7])
            elif e < 13:
                tiles.append(lane_roll(sz[e - 10], 1))
            elif e < 15:
                cond = dot3(sz, sz) / (0.5 * (vol + lane_roll(vol, -1)))
                tiles.append(cond if e == 13 else lane_roll(cond, 1))
            else:
                tiles.append(WALL_COEFF * vol / (mv[10, p] * mv[10, p]))
        for b, tile in enumerate(swap_segments(m, tiles)):
            ms[b, quad] = tile

    def pack(j):
        load_x(j).wait()
        low = [None] * 4
        high = [None] * 4
        for q in range(TILES):
            f, p = divmod(q, 2)
            tiles = swap_segments(m, [xv[j, f, p, 8 * y : 8 * y + 8, :] for y in range(4)])
            for b in range(4):
                sbuf[b, j, q] = tiles[b]
                low[b] = pack_edge(m, low[b], tiles[b], q, 0)
                high[b] = pack_edge(m, high[b], tiles[b], q, 30)
        for b in range(4):
            sbuf[(b + 1) % 4, j, TILES] = high[b]
            sbuf[(b + 3) % 4, j, TILES + 1] = low[b]

    def met_copy(k):
        return remote(ms.at[group(k)], mr.at[t], met_s.at[k - 1], met_r.at[k - 1], (group(k), s))

    def met_arrival(k):
        return remote(ms.at[t], mr.at[group(4 - k)], met_s.at[k - 1], met_r.at[k - 1], (group(k), s))

    def xin_copy(k, j):
        return remote(
            sbuf.at[group(k), j], region.at[t * PER + j],
            xin_s.at[k - 1, j], xin_r.at[k - 1, j], (group(k), s),
        )

    def xin_arrival(k, j):
        return remote(
            sbuf.at[t, j], region.at[group(4 - k) * PER + j],
            xin_s.at[k - 1, j], xin_r.at[k - 1, j], (group(k), s),
        )

    def forward(src, i):
        return (
            remote(src, hl0.at[i], fw_s.at[0, i], fw_r.at[0, i], right),
            remote(src, hr0.at[i], fw_s.at[1, i], fw_r.at[1, i], left),
        )

    def own_copy(j):
        return pltpu.make_async_copy(sbuf.at[t, j], region.at[t * PER + j], own_sem.at[j])

    mr[t] = ms[t]
    pl.semaphore_wait(barrier, 5)
    for k in (2, 1, 3):
        met_copy(k).start()

    @pl.loop(0, PER)
    def _(j):
        pack(j)
        for k in (2, 1, 3):
            xin_copy(k, j).start()
        for c in forward(sbuf.at[t, j, pl.ds(0, TILES)], t * PER + j):
            c.start()
        own_copy(j).start()

    for k in (2, 1, 3):
        met_arrival(k).wait_recv()
    for quad in range(8):
        for e, tile in enumerate(swap_segments(m, [mr[b, quad] for b in range(4)])):
            mt[4 * quad + e] = tile
    plane_metrics = (
        remote(mt.at[pl.ds(16, 4)], mleft, pm_s.at[0], pm_r.at[0], right),
        remote(mt.at[pl.ds(3, 1)], mright, pm_s.at[1], pm_r.at[1], left),
    )
    for c in plane_metrics:
        c.start()
    for p in range(2):
        o = 16 * p
        vol = mt[o + 3]
        sy = [mt[o + 4 + c] for c in range(3)]
        geo_y = geometry(sy, vol, y_up(m, vol, lane_roll(vol, -32), 1))
        geo_z = geometry_known([mt[o + 7 + c] for c in range(3)], mt[o + 13])
        geo_l = geometry_known([mt[o + 10 + c] for c in range(3)], mt[o + 14])
        for c in range(5):
            gy[p, c] = geo_y[c]
            gz[p, 0, c] = geo_z[c]
            gz[p, 1, c] = geo_l[c]

    def cross(i, w_of, low_pack, high_pack, first):
        for p in range(2):
            w = [w_of(f, p) for f in range(6)]
            prim = primitives(w)

            up = [y_up(m, w[f], lane_roll(w[f], -32), 1) for f in range(6)]
            flux, rad, sc = face(
                w, up,
                lambda f: y_up(m, w[f], lane_roll(w[f], -32), 2) - y_down(m, w[f], 1),
                prim, primitives(up), [gy[p, c] for c in range(5)], None if first else ry[i, p],
            )
            total = [flux[f] - y_down(m, flux[f], 1) for f in range(6)]
            total[5] = total[5] + mt[16 * p + 15] * w[5] * w[5] / w[0]
            if first:
                ry[i, p] = sc
                radii = rad + y_down(m, rad, 1) + 8.0 * mt[16 * p + 3]

            above = [lane_roll(high_pack, 32 - 2 * (2 * f + p)) for f in range(6)]
            below = [lane_roll(low_pack, -2 - 2 * (2 * f + p)) for f in range(6)]
            up = [lane_roll(jnp.where(m.zlo == 0, above[f], w[f]), -1) for f in range(6)]
            down = [lane_roll(jnp.where(m.zlo == 31, below[f], w[f]), 1) for f in range(6)]
            flux, rad, sc = face(
                w, up,
                lambda f: lane_roll(jnp.where(m.zlo < 2, above[f], w[f]), -2) - down[f],
                prim, primitives(up), [gz[p, 0, c] for c in range(5)], None if first else rz[i, p, 0],
            )
            total = [total[f] + flux[f] for f in range(6)]
            if first:
                rz[i, p, 0] = sc
                radii = radii + rad
            flux, rad, sc = face(
                down, w,
                lambda f: up[f] - lane_roll(jnp.where(m.zlo >= 30, below[f], w[f]), 2),
                primitives(down), prim, [gz[p, 1, c] for c in range(5)], None if first else rz[i, p, 1],
            )
            if first:
                rz[i, p, 1] = sc
                den[i, p] = radii + rad
            for f in range(6):
                r = total[f] - flux[f]
                if not first:
                    r = r + res[i, 2 * f + p]
                res[i, 2 * f + p] = r

    def mix(w_of, first):
        pc = [0.5 * (table_entry(d) + table_entry(d - 8)) for d in range(5)]
        qc = [0.5 * (table_entry(d) - table_entry(d - 8)) for d in range(5)]

        @pl.loop(0, TILES)
        def _(q):
            vol = mt[lax.rem(q, 2) * 16 + 3]
            w = [w_of(i, q) for i in range(NINST)]
            b = [w[i] + w[i + 8] for i in range(8)]
            a = [w[i] - w[i + 8] for i in range(8)]
            a = a + [-x for x in a]
            for r in range(8):
                even = None
                odd = qc[4] * a[(r - 4) % 16]
                for d in range(1, 4):
                    e = pc[d] * (b[(r - d) % 8] - b[(r + d) % 8])
                    even = e if even is None else even + e
                    odd = odd + qc[d] * (a[(r - d) % 16] - a[(r + d) % 16])
                for i, v in ((r, even + odd), (r + 8, even - odd)):
                    v = vol * v
                    res[i, q] = res[i, q] + v if first else v

    def axial(i, w_of, hl, hr, first):
        planes = [
            [hl[i, 2 * f] for f in range(6)],
            [hl[i, 2 * f + 1] for f in range(6)],
            [w_of(f, 0) for f in range(6)],
            [w_of(f, 1) for f in range(6)],
            [hr[i, 2 * f] for f in range(6)],
            [hr[i, 2 * f + 1] for f in range(6)],
        ]
        prims = [primitives(w) for w in planes[1:5]]
        fluxes, radii = [], []
        for k in range(3):
            geo = [gx[k, c] for c in range(5)]
            fx, rad, sc = face(
                planes[k + 1], planes[k + 2], lambda f, k=k: planes[k + 3][f] - planes[k][f],
                prims[k], prims[k + 1], geo, None if first else rx[i, k],
            )
            if first:
                rx[i, k] = sc
            fluxes.append(fx)
            radii.append(rad)
        if first:
            for p in range(2):
                step[i, p] = 0.5 / (den[i, p] + radii[p] + radii[p + 1])
        return [[fluxes[p + 1][f] - fluxes[p][f] for f in range(6)] for p in range(2)]

    def arrival_order(n):
        far = jnp.maximum(n - PER, 0)
        own = n < PER
        j = jnp.where(own, n, far // 3)
        back = jnp.where(own, 0, lax.rem(far, 3) + 1)
        return j, lax.rem(t + nt - back, nt) * PER + j

    def block_order(n):
        return n // 4, lax.rem(t + nt - lax.rem(n, 4), nt) * PER + n // 4

    def plane_copies(i):
        return (
            remote(w1.at[i], hl1.at[i], wp_s.at[0, i], wp_r.at[0, i], right),
            remote(w1.at[i], hr1.at[i], wp_s.at[1, i], wp_r.at[1, i], left),
        )

    def column_copies(i):
        return (
            remote(zs.at[i, 0], z1.at[i, 1], z_s.at[0, i], z_r.at[0, i], (group(3), s)),
            remote(zs.at[i, 1], z1.at[i, 0], z_s.at[1, i], z_r.at[1, i], (group(1), s)),
        )

    def receive_block(j):
        sources = [(k, lax.rem(t + nt - k, nt) * PER + j) for k in (1, 3, 2)]
        for k, i in sources:
            xin_arrival(k, j).wait_recv()
            for c in forward(region.at[i, pl.ds(0, TILES)], i):
                c.start()

    def face_metrics():
        for c in plane_metrics:
            c.wait_recv()
        sx = [[mleft[c] for c in range(3)], [mt[c] for c in range(3)], [mt[16 + c] for c in range(3)]]
        vx = [mleft[3], mt[3], mt[19], mright[0]]
        for k in range(3):
            for c, g in enumerate(geometry(sx[k], vx[k], vx[k + 1])):
                gx[k, c] = g

    @pl.loop(0, 2 * NINST)
    def _(n):
        k = n - NINST

        @pl.when(n < NINST)
        def _():
            j, i = arrival_order(n)

            @pl.when(n < PER)
            def _():
                own_copy(j).wait()

            @pl.when((n >= PER) & (lax.rem(jnp.maximum(n - PER, 0), 3) == 0))
            def _():
                receive_block(j)

            cross(i, lambda f, p: region[i, 2 * f + p], region[i, TILES], region[i, TILES + 1], True)

        @pl.when(n == LAG)
        def _():
            face_metrics()

        @pl.when(k == 0)
        def _():
            mix(lambda i, q: region[i, q], True)

        late = (k >= 2 * PER) & (lax.rem(n, 4) != 0)

        @pl.when(((n >= LAG) & (n < NINST)) | late)
        def _():
            i = jnp.where(n < NINST, arrival_order(n - LAG)[1], block_order(jnp.maximum(k, 0))[1])
            for c in forward(region.at[i, pl.ds(0, TILES)], i):
                c.wait_recv()
            change = axial(i, lambda f, p: region[i, 2 * f + p], hl0, hr0, True)
            for p in range(2):
                for f in range(6):
                    res[i, 2 * f + p] = res[i, 2 * f + p] + change[p][f]

        @pl.when(k >= 0)
        def _():
            j, i = block_order(jnp.maximum(k, 0))
            low = high = None
            for q in range(TILES):
                v = region[i, q] - 0.5 * step[i, q % 2] * res[i, q]
                w1[i, q] = v
                low = pack_edge(m, low, v, q, 0)
                high = pack_edge(m, high, v, q, 30)
            zs[i, 0] = low
            zs[i, 1] = high
            for c in plane_copies(i) + column_copies(i):
                c.start()

    mix(lambda i, q: w1[i, q], False)

    def out_copy(k, j):
        g = group(k)
        return remote(
            ob.at[g * PER + j], oin.at[t, j], o_s.at[k - 1, j], o_r.at[k - 1, j], (g, s)
        )

    def out_arrival(k, j):
        return remote(
            ob.at[t * PER + j], oin.at[group(4 - k), j],
            o_s.at[k - 1, j], o_r.at[k - 1, j], (group(k), s),
        )

    def store_out(j):
        return pltpu.make_async_copy(ov.at[j], out.at[j], out_sem.at[j])

    @pl.loop(0, NINST)
    def _(n):
        j, i = block_order(n)
        back = lax.rem(n, 4)
        for c in column_copies(i):
            c.wait_recv()
        cross(i, lambda f, p: w1[i, 2 * f + p], z1[i, 0], z1[i, 1], False)
        for c in plane_copies(i):
            c.wait_recv()
        change = axial(i, lambda f, p: w1[i, 2 * f + p], hl1, hr1, False)
        for p in range(2):
            for f in range(6):
                ob[i, 2 * f + p] = -step[i, p] * (res[i, 2 * f + p] + change[p][f])

        @pl.when(back > 0)
        def _():
            out_copy(4 - back, j).start()

        @pl.when(back == 0)
        def _():
            for q in range(TILES):
                oin[t, j, q] = ob[i, q]

    @pl.loop(0, PER)
    def _(j):
        for k in range(1, 4):
            out_arrival(k, j).wait_recv()
        for q in range(TILES):
            f, p = divmod(q, 2)
            tiles = swap_segments(m, [oin[b, j, q] for b in range(4)])
            for y in range(4):
                ov[j, f, p, 8 * y : 8 * y + 8, :] = tiles[y]
        store_out(j).start()

    for k in (1, 2, 3):
        met_copy(k).wait_send()
    for c in plane_metrics:
        c.wait_send()

    @pl.loop(0, PER)
    def _(j):
        for k in (1, 2, 3):
            xin_copy(k, j).wait_send()
            out_copy(k, j).wait_send()

    @pl.loop(0, NINST)
    def _(i):
        for c in forward(region.at[i, pl.ds(0, TILES)], i):
            c.wait_send()
        for c in plane_copies(i) + column_copies(i):
            c.wait_send()

    for j in range(PER):
        store_out(j).wait()


def per_device(flow_state, metrics):
    tile = (8, 128)
    f32 = jnp.float32

    def vmem(*lead):
        return pltpu.VMEM(lead + tile, f32)

    dma = pltpu.SemaphoreType.DMA
    full = (NINST, TILES)
    return pl.pallas_call(
        kernel,
        out_shape=jax.ShapeDtypeStruct(flow_state.shape, f32),
        in_specs=[pl.BlockSpec(memory_space=pl.ANY)] * 2,
        out_specs=pl.BlockSpec(memory_space=pl.ANY),
        scratch_shapes=[
            pltpu.VMEM(flow_state.shape, f32),
            pltpu.VMEM(metrics.shape, f32),
            vmem(GROUPS, PER, TILES + 2),
            vmem(NINST, TILES + 2),
            vmem(*full),
            vmem(*full),
            vmem(*full),
            vmem(*full),
            vmem(NINST, 2),
            vmem(NINST, 2),
            vmem(*full),
            vmem(*full),
            vmem(*full),
            vmem(GROUPS, PER, TILES),
            pltpu.VMEM(flow_state.shape, f32),
            vmem(4, 8),
            vmem(4, 8),
            vmem(32),
            vmem(4),
            vmem(1),
            vmem(3, 5),
            vmem(2, 5),
            vmem(2, 2, 5),
            vmem(NINST, 2),
            vmem(NINST, 2, 2),
            vmem(NINST, 3),
            vmem(NINST, 2),
            vmem(NINST, 2),
            dma((PER + 1,)),
            dma((PER,)),
            dma((PER,)),
            dma((3,)),
            dma((3,)),
            dma((2,)),
            dma((2,)),
            dma((3, PER)),
            dma((3, PER)),
            dma((2, NINST)),
            dma((2, NINST)),
            dma((2, NINST)),
            dma((2, NINST)),
            dma((2, NINST)),
            dma((2, NINST)),
            dma((3, PER)),
            dma((3, PER)),
        ],
        compiler_params=pltpu.CompilerParams(
            collective_id=0, has_side_effects=True, vmem_limit_bytes=53 << 20
        ),
        cost_estimate=pl.CostEstimate(
            flops=100_000_000, bytes_accessed=1_800_000, transcendentals=200_000
        ),
        name="balance",
    )(flow_state, metrics)


def solution(mesh):
    return jax.shard_map(
        per_device,
        mesh=mesh,
        in_specs=(P("tm", None, "space", None, None), P(None, "space", "tm", None)),
        out_specs=P("tm", None, "space", None, None),
        check_vma=False,
    )
```

```python
import math

import jax
import jax.numpy as jnp
from jax import lax
from jax.experimental import pallas as pl
from jax.experimental.pallas import tpu as pltpu
from jax.sharding import PartitionSpec as P

NINST = 16
GROUPS = 4
PER = 4
TILES = 12
LAG = 9
AHEAD = 8
GAMMA = 1.4
EPS_TWO = 0.1
EPS_FOUR = 0.03125
JUMP_RATIO = (EPS_TWO + 3.0 * EPS_FOUR) / EPS_FOUR
VISCOSITY = 0.02
HEAT_FACTOR = 1.4 / (0.4 * 0.72)
TURB_DIFFUSE = 1.5
WALL_COEFF = 3.24
MESH = pl.DeviceIdType.MESH


def table_entry(offset):
    offset = offset % NINST
    if offset == 0 or offset == NINST // 2:
        return 0.0
    parity = 1.0 if offset % 2 == 0 else -1.0
    return 0.5 * parity / math.tan(math.pi * offset / NINST)


def lane_roll(x, k):
    k = k % 128
    return x if k == 0 else pltpu.roll(x, k, 1)


def row_roll(x, k):
    k = k % 8
    return x if k == 0 else pltpu.roll(x, k, 0)


class Masks:
    def __init__(self):
        lane = lax.broadcasted_iota(jnp.int32, (8, 128), 1)
        self.row = lax.broadcasted_iota(jnp.int32, (8, 128), 0)
        self.zlo = lane & 31
        self.pair = self.zlo >> 1
        self.half = lane < 64
        self.even = (lane & 32) == 0


def swap_segments(m, x):
    a0 = jnp.where(m.half, x[0], lane_roll(x[2], 64))
    a2 = jnp.where(m.half, lane_roll(x[0], 64), x[2])
    a1 = jnp.where(m.half, x[1], lane_roll(x[3], 64))
    a3 = jnp.where(m.half, lane_roll(x[1], 64), x[3])
    return [
        jnp.where(m.even, a0, lane_roll(a1, 32)),
        jnp.where(m.even, lane_roll(a0, -32), a1),
        jnp.where(m.even, a2, lane_roll(a3, 32)),
        jnp.where(m.even, lane_roll(a2, -32), a3),
    ]


def pack_edges(m, low, high, moved, k):
    low = moved if low is None else jnp.where(m.pair == k, moved, low)
    high = moved if high is None else jnp.where(m.pair == (k - 1) % 16, moved, high)
    return low, high


def y_up(m, w, w32, k):
    return row_roll(jnp.where(m.row < k, w32, w), -k)


def y_down(m, w, k):
    return row_roll(jnp.where(m.row >= 8 - k, lane_roll(w, 32), w), k)


def primitives(w):
    inv = 1.0 / w[0]
    u = [w[1] * inv, w[2] * inv, w[3] * inv]
    kin = 0.5 * (w[1] * u[0] + w[2] * u[1] + w[3] * u[2])
    p = (GAMMA - 1.0) * (w[4] - kin)
    temp = p * inv
    return dict(
        u=u,
        p=p,
        h=w[4] + p,
        e=kin * inv + HEAT_FACTOR * temp,
        n=TURB_DIFFUSE * (w[5] * inv),
        t=temp,
    )


def half_sound(prim):
    return 0.5 * jnp.sqrt(GAMMA * prim["t"])


def dot3(a, b):
    return a[0] * b[0] + a[1] * b[1] + a[2] * b[2]


def face(wl, wr, outer, pl_, pr_, geo, scaled=None):
    hs, length, cond = geo[0:3], geo[3], geo[4]
    ql = dot3(pl_["u"], hs)
    qr = dot3(pr_["u"], hs)
    rad = None
    if scaled is None:
        rad = jnp.abs(ql + qr) + (half_sound(pl_) + half_sound(pr_)) * length
        scaled = EPS_FOUR * rad
    g = (VISCOSITY + 0.5 * (wl[5] + wr[5])) * cond
    psum = pl_["p"] + pr_["p"]
    out = []
    for f in range(6):
        if f == 4:
            c = pl_["h"] * ql + pr_["h"] * qr
        else:
            c = wl[f] * ql + wr[f] * qr
        if 1 <= f <= 3:
            c = c + psum * hs[f - 1] - g * (pr_["u"][f - 1] - pl_["u"][f - 1])
        if f == 4:
            c = c - g * (pr_["e"] - pl_["e"])
        if f == 5:
            c = c - g * (pr_["n"] - pl_["n"])
        d = wr[f] - wl[f]
        out.append(c - scaled * (JUMP_RATIO * d - outer(f)))
    return out, rad, scaled


def geometry(s, left_volume, right_volume):
    sq = dot3(s, s)
    return [0.5 * s[0], 0.5 * s[1], 0.5 * s[2], jnp.sqrt(sq), sq / (0.5 * (left_volume + right_volume))]


def geometry_known(s, cond):
    return [0.5 * s[0], 0.5 * s[1], 0.5 * s[2], jnp.sqrt(dot3(s, s)), cond]


def kernel(
    flow, metrics, out,
    xv, mv, sbuf, region, hl0, hr0, res, coupling, w1, moved1, zs, z1, hl1, hr1, ob, oin, ov,
    ms, mr, mt, mleft, mright, gx, gy, gz, ry, rz, rx, den, step,
    in_sem, own_sem, out_sem, met_s, met_r, pm_s, pm_r,
    go, xin_s, xin_r, fw_s, fw_r, wp_s, wp_r, z_s, z_r, o_s, o_r,
):
    t = lax.axis_index("tm")
    s = lax.axis_index("space")
    nt = lax.axis_size("tm")
    ns = lax.axis_size("space")
    right = (t, lax.rem(s + 1, ns))
    left = (t, lax.rem(s + ns - 1, ns))
    upper = lax.rem(s, 2) == 1

    def group(k):
        return lax.rem(t + k, nt)

    def remote(src, dst, ss, rs, dev):
        return pltpu.make_async_remote_copy(
            src_ref=src, dst_ref=dst, send_sem=ss, recv_sem=rs, device_id=dev, device_id_type=MESH
        )

    barrier = pltpu.get_barrier_semaphore()
    for dev in ((group(1), s), (group(2), s), (group(3), s), left, right):
        pl.semaphore_signal(barrier, inc=1, device_id=dev, device_id_type=MESH)

    load_m = pltpu.make_async_copy(metrics, mv, in_sem.at[PER])
    load_m.start()

    def load_x(j):
        return pltpu.make_async_copy(flow.at[j], xv.at[j], in_sem.at[j])

    for j in range(PER):
        load_x(j).start()

    m = Masks()
    load_m.wait()
    for quad in range(8):
        tiles = []
        for e in range(4 * quad, 4 * quad + 4):
            p, e = divmod(e, 16)
            sz = [mv[6 + c, p] for c in range(3)]
            vol = mv[9, p]
            if e < 3:
                tiles.append(mv[e, p])
            elif e == 3:
                tiles.append(vol)
            elif e < 7:
                tiles.append(mv[e - 1, p])
            elif e < 10:
                tiles.append(sz[e - 7])
            elif e < 13:
                tiles.append(lane_roll(sz[e - 10], 1))
            elif e < 15:
                cond = dot3(sz, sz) / (0.5 * (vol + lane_roll(vol, -1)))
                tiles.append(cond if e == 13 else lane_roll(cond, 1))
            else:
                tiles.append(WALL_COEFF * vol / (mv[10, p] * mv[10, p]))
        for b, tile in enumerate(swap_segments(m, tiles)):
            ms[b, quad] = tile

    def pack(j):
        load_x(j).wait()
        low = [None] * 4
        high = [None] * 4
        for q in range(TILES):
            f, p = divmod(q, 2)
            tiles = swap_segments(m, [xv[j, f, p, 8 * y : 8 * y + 8, :] for y in range(4)])
            for b in range(4):
                sbuf[b, j, q] = tiles[b]
                low[b], high[b] = pack_edges(m, low[b], high[b], lane_roll(tiles[b], 2 * q), q)
        for b in range(4):
            sbuf[(b + 1) % 4, j, TILES] = lane_roll(high[b], -32)
            sbuf[(b + 3) % 4, j, TILES + 1] = lane_roll(low[b], 32)

    def met_copy(k):
        return remote(ms.at[group(k)], mr.at[t], met_s.at[k - 1], met_r.at[k - 1], (group(k), s))

    def met_arrival(k):
        return remote(ms.at[t], mr.at[group(4 - k)], met_s.at[k - 1], met_r.at[k - 1], (group(k), s))

    def xin_copy(k, j):
        return remote(
            sbuf.at[group(k), j], region.at[t * PER + j],
            xin_s.at[k - 1, j], xin_r.at[k - 1, j], (group(k), s),
        )

    def xin_arrival(k, j):
        return remote(
            sbuf.at[t, j], region.at[group(4 - k) * PER + j],
            xin_s.at[k - 1, j], xin_r.at[k - 1, j], (group(k), s),
        )

    def forward(src, i):
        return (
            remote(src, hl0.at[i], fw_s.at[0, i], fw_r.at[0, i], right),
            remote(src, hr0.at[i], fw_s.at[1, i], fw_r.at[1, i], left),
        )

    def own_copy(j):
        return pltpu.make_async_copy(sbuf.at[t, j], region.at[t * PER + j], own_sem.at[j])

    mr[t] = ms[t]
    pl.semaphore_wait(barrier, 5)
    for k in (2, 1, 3):
        met_copy(k).start()

    @pl.loop(0, PER)
    def _(j):
        pack(j)

        @pl.when(upper)
        def _():
            for k in (2, 1, 3):
                xin_copy(k, j).start()

        for c in forward(sbuf.at[t, j, pl.ds(0, TILES)], t * PER + j):
            c.start()
        own_copy(j).start()

    @pl.when(upper)
    def _():
        pl.semaphore_signal(go, inc=1, device_id=left, device_id_type=MESH)

    @pl.when(jnp.logical_not(upper))
    def _():
        pl.semaphore_wait(go, 1)
        for j in range(PER):
            for k in (2, 1, 3):
                xin_copy(k, j).start()

    for k in (2, 1, 3):
        met_arrival(k).wait_recv()
    for quad in range(8):
        for e, tile in enumerate(swap_segments(m, [mr[b, quad] for b in range(4)])):
            mt[4 * quad + e] = tile
    plane_metrics = (
        remote(mt.at[pl.ds(16, 4)], mleft, pm_s.at[0], pm_r.at[0], right),
        remote(mt.at[pl.ds(3, 1)], mright, pm_s.at[1], pm_r.at[1], left),
    )
    for c in plane_metrics:
        c.start()
    for p in range(2):
        o = 16 * p
        vol = mt[o + 3]
        sy = [mt[o + 4 + c] for c in range(3)]
        geo_y = geometry(sy, vol, y_up(m, vol, lane_roll(vol, -32), 1))
        geo_z = geometry_known([mt[o + 7 + c] for c in range(3)], mt[o + 13])
        geo_l = geometry_known([mt[o + 10 + c] for c in range(3)], mt[o + 14])
        for c in range(5):
            gy[p, c] = geo_y[c]
            gz[p, 0, c] = geo_z[c]
            gz[p, 1, c] = geo_l[c]

    def cross(i, w_of, moved_of, low_pack, high_pack, first):
        for p in range(2):
            w = [w_of(f, p) for f in range(6)]
            prim = primitives(w)

            up = [y_up(m, w[f], lane_roll(w[f], -32), 1) for f in range(6)]
            flux, rad, sc = face(
                w, up,
                lambda f: y_up(m, w[f], lane_roll(w[f], -32), 2) - y_down(m, w[f], 1),
                prim, primitives(up), [gy[p, c] for c in range(5)], None if first else ry[i, p],
            )
            total = [flux[f] - y_down(m, flux[f], 1) for f in range(6)]
            total[5] = total[5] + mt[16 * p + 15] * w[5] * w[5] / w[0]
            if first:
                ry[i, p] = sc
                radii = rad + y_down(m, rad, 1) + 8.0 * mt[16 * p + 3]

            moved = [moved_of(f, p) for f in range(6)]
            at = [2 * f + p for f in range(6)]

            def shifted(f, mask, pack, k):
                return lane_roll(jnp.where(mask, pack, moved[f]), k - 2 * at[f])

            up = [shifted(f, m.zlo == 2 * at[f], high_pack, -1) for f in range(6)]
            down = [shifted(f, m.zlo == (2 * at[f] - 1) % 32, low_pack, 1) for f in range(6)]
            flux, rad, sc = face(
                w, up,
                lambda f: shifted(f, m.pair == at[f], high_pack, -2) - down[f],
                prim, primitives(up), [gz[p, 0, c] for c in range(5)], None if first else rz[i, p, 0],
            )
            total = [total[f] + flux[f] for f in range(6)]
            if first:
                rz[i, p, 0] = sc
                radii = radii + rad
            flux, rad, sc = face(
                down, w,
                lambda f: up[f] - shifted(f, m.pair == (at[f] - 1) % 16, low_pack, 2),
                primitives(down), prim, [gz[p, 1, c] for c in range(5)], None if first else rz[i, p, 1],
            )
            if first:
                rz[i, p, 1] = sc
                den[i, p] = radii + rad
            for f in range(6):
                res[i, 2 * f + p] = total[f] - flux[f]

    def mix(w_of, first):
        pc = [0.5 * (table_entry(d) + table_entry(d - 8)) for d in range(5)]
        qc = [0.5 * (table_entry(d) - table_entry(d - 8)) for d in range(5)]

        @pl.loop(0, TILES)
        def _(q):
            vol = mt[lax.rem(q, 2) * 16 + 3]
            w = [w_of(i, q) for i in range(NINST)]
            b = [w[i] + w[i + 8] for i in range(8)]
            a = [w[i] - w[i + 8] for i in range(8)]
            a = a + [-x for x in a]
            for r in range(8):
                even = None
                odd = qc[4] * a[(r - 4) % 16]
                for d in range(1, 4):
                    e = pc[d] * (b[(r - d) % 8] - b[(r + d) % 8])
                    even = e if even is None else even + e
                    odd = odd + qc[d] * (a[(r - d) % 16] - a[(r + d) % 16])
                for i, v in ((r, even + odd), (r + 8, even - odd)):
                    v = vol * v
                    if first:
                        res[i, q] = res[i, q] + v
                    else:
                        coupling[i, q] = v

    def axial(i, w_of, hl, hr, first):
        planes = [
            [hl[i, 2 * f] for f in range(6)],
            [hl[i, 2 * f + 1] for f in range(6)],
            [w_of(f, 0) for f in range(6)],
            [w_of(f, 1) for f in range(6)],
            [hr[i, 2 * f] for f in range(6)],
            [hr[i, 2 * f + 1] for f in range(6)],
        ]
        prims = [primitives(w) for w in planes[1:5]]
        fluxes, radii = [], []
        for k in range(3):
            geo = [gx[k, c] for c in range(5)]
            fx, rad, sc = face(
                planes[k + 1], planes[k + 2], lambda f, k=k: planes[k + 3][f] - planes[k][f],
                prims[k], prims[k + 1], geo, None if first else rx[i, k],
            )
            if first:
                rx[i, k] = sc
            fluxes.append(fx)
            radii.append(rad)
        if first:
            for p in range(2):
                step[i, p] = 0.5 / (den[i, p] + radii[p] + radii[p + 1])
        return [[fluxes[p + 1][f] - fluxes[p][f] for f in range(6)] for p in range(2)]

    def arrival_order(n):
        far = jnp.maximum(n - PER, 0)
        own = n < PER
        j = jnp.where(own, n, far // 3)
        back = jnp.where(own, 0, lax.rem(far, 3) + 1)
        return j, lax.rem(t + nt - back, nt) * PER + j

    def block_order(n):
        return n // 4, lax.rem(t + nt - lax.rem(n, 4), nt) * PER + n // 4

    def plane_copies(i):
        return (
            remote(w1.at[i], hl1.at[i], wp_s.at[0, i], wp_r.at[0, i], right),
            remote(w1.at[i], hr1.at[i], wp_s.at[1, i], wp_r.at[1, i], left),
        )

    def column_copies(i):
        return (
            remote(zs.at[i, 0], z1.at[i, 1], z_s.at[0, i], z_r.at[0, i], (group(3), s)),
            remote(zs.at[i, 1], z1.at[i, 0], z_s.at[1, i], z_r.at[1, i], (group(1), s)),
        )

    def receive_block(j):
        sources = [(k, lax.rem(t + nt - k, nt) * PER + j) for k in (1, 3, 2)]
        for k, i in sources:
            xin_arrival(k, j).wait_recv()
            for c in forward(region.at[i, pl.ds(0, TILES)], i):
                c.start()

    def face_metrics():
        for c in plane_metrics:
            c.wait_recv()
        sx = [[mleft[c] for c in range(3)], [mt[c] for c in range(3)], [mt[16 + c] for c in range(3)]]
        vx = [mleft[3], mt[3], mt[19], mright[0]]
        for k in range(3):
            for c, g in enumerate(geometry(sx[k], vx[k], vx[k + 1])):
                gx[k, c] = g

    def second_cross(i):
        for c in column_copies(i):
            c.wait_recv()
        cross(
            i,
            lambda f, p: w1[i, 2 * f + p],
            lambda f, p: moved1[i, 2 * f + p],
            z1[i, 0], z1[i, 1], False,
        )

    @pl.loop(0, 2 * NINST)
    def _(n):
        k = n - NINST

        @pl.when(n < NINST)
        def _():
            j, i = arrival_order(n)

            @pl.when(n < PER)
            def _():
                own_copy(j).wait()

            @pl.when((n >= PER) & (lax.rem(jnp.maximum(n - PER, 0), 3) == 0))
            def _():
                receive_block(j)

            cross(
                i,
                lambda f, p: region[i, 2 * f + p],
                lambda f, p: lane_roll(region[i, 2 * f + p], 2 * (2 * f + p)),
                region[i, TILES], region[i, TILES + 1], True,
            )

        @pl.when(n == LAG)
        def _():
            face_metrics()

        @pl.when(k == 0)
        def _():
            mix(lambda i, q: region[i, q], True)

        @pl.when(k >= AHEAD)
        def _():
            second_cross(block_order(jnp.maximum(k - AHEAD, 0))[1])

        late = (k >= PER) & (lax.rem(n, 4) != 0)

        @pl.when(((n >= LAG) & (n < NINST)) | late)
        def _():
            i = jnp.where(n < NINST, arrival_order(n - LAG)[1], block_order(jnp.maximum(k, 0))[1])
            for c in forward(region.at[i, pl.ds(0, TILES)], i):
                c.wait_recv()
            change = axial(i, lambda f, p: region[i, 2 * f + p], hl0, hr0, True)
            for p in range(2):
                for f in range(6):
                    res[i, 2 * f + p] = res[i, 2 * f + p] + change[p][f]

        @pl.when(k >= 0)
        def _():
            j, i = block_order(jnp.maximum(k, 0))
            low = high = None
            for q in range(TILES):
                v = region[i, q] - 0.5 * step[i, q % 2] * res[i, q]
                w1[i, q] = v
                moved = lane_roll(v, 2 * q)
                moved1[i, q] = moved
                low, high = pack_edges(m, low, high, moved, q)
            zs[i, 0] = lane_roll(low, 32)
            zs[i, 1] = lane_roll(high, -32)
            for c in plane_copies(i) + column_copies(i):
                c.start()

    mix(lambda i, q: w1[i, q], False)

    def out_copy(k, j):
        g = group(k)
        return remote(
            ob.at[g * PER + j], oin.at[t, j], o_s.at[k - 1, j], o_r.at[k - 1, j], (g, s)
        )

    def out_arrival(k, j):
        return remote(
            ob.at[t * PER + j], oin.at[group(4 - k), j],
            o_s.at[k - 1, j], o_r.at[k - 1, j], (group(k), s),
        )

    def store_out(j):
        return pltpu.make_async_copy(ov.at[j], out.at[j], out_sem.at[j])

    @pl.loop(0, NINST)
    def _(n):
        j, i = block_order(n)
        back = lax.rem(n, 4)

        @pl.when(n >= NINST - AHEAD)
        def _():
            second_cross(i)

        for c in plane_copies(i):
            c.wait_recv()
        change = axial(i, lambda f, p: w1[i, 2 * f + p], hl1, hr1, False)
        for p in range(2):
            for f in range(6):
                ob[i, 2 * f + p] = -step[i, p] * (res[i, 2 * f + p] + coupling[i, 2 * f + p] + change[p][f])

        @pl.when(back > 0)
        def _():
            out_copy(4 - back, j).start()

        @pl.when(back == 0)
        def _():
            for q in range(TILES):
                oin[t, j, q] = ob[i, q]

    @pl.loop(0, PER)
    def _(j):
        for k in range(1, 4):
            out_arrival(k, j).wait_recv()
        for q in range(TILES):
            f, p = divmod(q, 2)
            tiles = swap_segments(m, [oin[b, j, q] for b in range(4)])
            for y in range(4):
                ov[j, f, p, 8 * y : 8 * y + 8, :] = tiles[y]
        store_out(j).start()

    for k in (1, 2, 3):
        met_copy(k).wait_send()
    for c in plane_metrics:
        c.wait_send()

    @pl.loop(0, PER)
    def _(j):
        for k in (1, 2, 3):
            xin_copy(k, j).wait_send()
            out_copy(k, j).wait_send()

    @pl.loop(0, NINST)
    def _(i):
        for c in forward(region.at[i, pl.ds(0, TILES)], i):
            c.wait_send()
        for c in plane_copies(i) + column_copies(i):
            c.wait_send()

    for j in range(PER):
        store_out(j).wait()


def per_device(flow_state, metrics):
    tile = (8, 128)
    f32 = jnp.float32

    def vmem(*lead):
        return pltpu.VMEM(lead + tile, f32)

    dma = pltpu.SemaphoreType.DMA
    full = (NINST, TILES)
    return pl.pallas_call(
        kernel,
        out_shape=jax.ShapeDtypeStruct(flow_state.shape, f32),
        in_specs=[pl.BlockSpec(memory_space=pl.ANY)] * 2,
        out_specs=pl.BlockSpec(memory_space=pl.ANY),
        scratch_shapes=[
            pltpu.VMEM(flow_state.shape, f32),
            pltpu.VMEM(metrics.shape, f32),
            vmem(GROUPS, PER, TILES + 2),
            vmem(NINST, TILES + 2),
            vmem(*full),
            vmem(*full),
            vmem(*full),
            vmem(*full),
            vmem(*full),
            vmem(*full),
            vmem(NINST, 2),
            vmem(NINST, 2),
            vmem(*full),
            vmem(*full),
            vmem(*full),
            vmem(GROUPS, PER, TILES),
            pltpu.VMEM(flow_state.shape, f32),
            vmem(4, 8),
            vmem(4, 8),
            vmem(32),
            vmem(4),
            vmem(1),
            vmem(3, 5),
            vmem(2, 5),
            vmem(2, 2, 5),
            vmem(NINST, 2),
            vmem(NINST, 2, 2),
            vmem(NINST, 3),
            vmem(NINST, 2),
            vmem(NINST, 2),
            dma((PER + 1,)),
            dma((PER,)),
            dma((PER,)),
            dma((3,)),
            dma((3,)),
            dma((2,)),
            dma((2,)),
            pltpu.SemaphoreType.REGULAR,
            dma((3, PER)),
            dma((3, PER)),
            dma((2, NINST)),
            dma((2, NINST)),
            dma((2, NINST)),
            dma((2, NINST)),
            dma((2, NINST)),
            dma((2, NINST)),
            dma((3, PER)),
            dma((3, PER)),
        ],
        compiler_params=pltpu.CompilerParams(
            collective_id=0, has_side_effects=True, vmem_limit_bytes=53 << 20
        ),
        cost_estimate=pl.CostEstimate(
            flops=100_000_000, bytes_accessed=1_800_000, transcendentals=200_000
        ),
        name="balance",
    )(flow_state, metrics)


def solution(mesh):
    return jax.shard_map(
        per_device,
        mesh=mesh,
        in_specs=(P("tm", None, "space", None, None), P(None, "space", "tm", None)),
        out_specs=P("tm", None, "space", None, None),
        check_vma=False,
    )
```

```python
import math

import jax
import jax.numpy as jnp
from jax import lax
from jax.experimental import pallas as pl
from jax.experimental.pallas import tpu as pltpu
from jax.sharding import PartitionSpec as P

NINST = 16
GROUPS = 4
PER = 4
TILES = 12
LAG = 9
AHEAD = 8
GAMMA = 1.4
EPS_TWO = 0.1
EPS_FOUR = 0.03125
JUMP_RATIO = (EPS_TWO + 3.0 * EPS_FOUR) / EPS_FOUR
VISCOSITY = 0.02
HEAT_FACTOR = 1.4 / (0.4 * 0.72)
TURB_DIFFUSE = 1.5
WALL_COEFF = 3.24
MESH = pl.DeviceIdType.MESH


def table_entry(offset):
    offset = offset % NINST
    if offset == 0 or offset == NINST // 2:
        return 0.0
    parity = 1.0 if offset % 2 == 0 else -1.0
    return 0.5 * parity / math.tan(math.pi * offset / NINST)


def lane_roll(x, k):
    k = k % 128
    return x if k == 0 else pltpu.roll(x, k, 1)


def row_roll(x, k):
    k = k % 8
    return x if k == 0 else pltpu.roll(x, k, 0)


class Masks:
    def __init__(self):
        lane = lax.broadcasted_iota(jnp.int32, (8, 128), 1)
        self.row = lax.broadcasted_iota(jnp.int32, (8, 128), 0)
        self.zlo = lane & 31
        self.pair = self.zlo >> 1
        self.half = lane < 64
        self.even = (lane & 32) == 0


def swap_segments(m, x):
    a0 = jnp.where(m.half, x[0], lane_roll(x[2], 64))
    a2 = jnp.where(m.half, lane_roll(x[0], 64), x[2])
    a1 = jnp.where(m.half, x[1], lane_roll(x[3], 64))
    a3 = jnp.where(m.half, lane_roll(x[1], 64), x[3])
    return [
        jnp.where(m.even, a0, lane_roll(a1, 32)),
        jnp.where(m.even, lane_roll(a0, -32), a1),
        jnp.where(m.even, a2, lane_roll(a3, 32)),
        jnp.where(m.even, lane_roll(a2, -32), a3),
    ]


def pack_edges(m, low, high, moved, k):
    low = moved if low is None else jnp.where(m.pair == k, moved, low)
    high = moved if high is None else jnp.where(m.pair == (k - 1) % 16, moved, high)
    return low, high


def y_up(m, w, w32, k):
    return row_roll(jnp.where(m.row < k, w32, w), -k)


def y_down(m, w, k):
    return row_roll(jnp.where(m.row >= 8 - k, lane_roll(w, 32), w), k)


def primitives(w):
    inv = 1.0 / w[0]
    u = [w[1] * inv, w[2] * inv, w[3] * inv]
    kin = 0.5 * (w[1] * u[0] + w[2] * u[1] + w[3] * u[2])
    p = (GAMMA - 1.0) * (w[4] - kin)
    temp = p * inv
    return dict(
        u=u,
        p=p,
        h=w[4] + p,
        e=kin * inv + HEAT_FACTOR * temp,
        n=TURB_DIFFUSE * (w[5] * inv),
        t=temp,
    )


def half_sound(prim):
    return 0.5 * jnp.sqrt(GAMMA * prim["t"])


def dot3(a, b):
    return a[0] * b[0] + a[1] * b[1] + a[2] * b[2]


def face(wl, wr, outer, pl_, pr_, geo, scaled=None):
    hs, length, cond = geo[0:3], geo[3], geo[4]
    ql = dot3(pl_["u"], hs)
    qr = dot3(pr_["u"], hs)
    rad = None
    if scaled is None:
        rad = jnp.abs(ql + qr) + (half_sound(pl_) + half_sound(pr_)) * length
        scaled = EPS_FOUR * rad
    g = (VISCOSITY + 0.5 * (wl[5] + wr[5])) * cond
    psum = pl_["p"] + pr_["p"]
    out = []
    for f in range(6):
        if f == 4:
            c = pl_["h"] * ql + pr_["h"] * qr
        else:
            c = wl[f] * ql + wr[f] * qr
        if 1 <= f <= 3:
            c = c + psum * hs[f - 1] - g * (pr_["u"][f - 1] - pl_["u"][f - 1])
        if f == 4:
            c = c - g * (pr_["e"] - pl_["e"])
        if f == 5:
            c = c - g * (pr_["n"] - pl_["n"])
        d = wr[f] - wl[f]
        out.append(c - scaled * (JUMP_RATIO * d - outer(f)))
    return out, rad, scaled


def geometry(s, left_volume, right_volume):
    sq = dot3(s, s)
    return [0.5 * s[0], 0.5 * s[1], 0.5 * s[2], jnp.sqrt(sq), sq / (0.5 * (left_volume + right_volume))]


def geometry_known(s, cond):
    return [0.5 * s[0], 0.5 * s[1], 0.5 * s[2], jnp.sqrt(dot3(s, s)), cond]


def kernel(
    flow, metrics, out,
    xv, mv, sbuf, region, hl0, hr0, res, coupling, w1, moved1, zs, z1, hl1, hr1, ob, oin, ov,
    ms, mr, mt, mleft, mright, gx, gy, gz, ry, rz, rx, den, step,
    in_sem, own_sem, out_sem, met_s, met_r, pm_s, pm_r,
    go, xin_s, xin_r, fw_s, fw_r, wp_s, wp_r, z_s, z_r, o_s, o_r,
):
    t = lax.axis_index("tm")
    s = lax.axis_index("space")
    nt = lax.axis_size("tm")
    ns = lax.axis_size("space")
    right = (t, lax.rem(s + 1, ns))
    left = (t, lax.rem(s + ns - 1, ns))
    upper = lax.rem(s, 2) == 1

    def group(k):
        return lax.rem(t + k, nt)

    def remote(src, dst, ss, rs, dev):
        return pltpu.make_async_remote_copy(
            src_ref=src, dst_ref=dst, send_sem=ss, recv_sem=rs, device_id=dev, device_id_type=MESH
        )

    barrier = pltpu.get_barrier_semaphore()
    for dev in ((group(1), s), (group(2), s), (group(3), s), left, right):
        pl.semaphore_signal(barrier, inc=1, device_id=dev, device_id_type=MESH)

    load_m = pltpu.make_async_copy(metrics, mv, in_sem.at[PER])
    load_m.start()

    def load_x(j):
        return pltpu.make_async_copy(flow.at[j], xv.at[j], in_sem.at[j])

    for j in range(PER):
        load_x(j).start()

    m = Masks()
    load_m.wait()
    for quad in range(8):
        tiles = []
        for e in range(4 * quad, 4 * quad + 4):
            p, e = divmod(e, 16)
            sz = [mv[6 + c, p] for c in range(3)]
            vol = mv[9, p]
            if e < 3:
                tiles.append(mv[e, p])
            elif e == 3:
                tiles.append(vol)
            elif e < 7:
                tiles.append(mv[e - 1, p])
            elif e < 10:
                tiles.append(sz[e - 7])
            elif e < 13:
                tiles.append(lane_roll(sz[e - 10], 1))
            elif e < 15:
                cond = dot3(sz, sz) / (0.5 * (vol + lane_roll(vol, -1)))
                tiles.append(cond if e == 13 else lane_roll(cond, 1))
            else:
                tiles.append(WALL_COEFF * vol / (mv[10, p] * mv[10, p]))
        for b, tile in enumerate(swap_segments(m, tiles)):
            ms[b, quad] = tile

    def pack(j):
        load_x(j).wait()
        low = [None] * 4
        high = [None] * 4
        for q in range(TILES):
            f, p = divmod(q, 2)
            tiles = swap_segments(m, [xv[j, f, p, 8 * y : 8 * y + 8, :] for y in range(4)])
            for b in range(4):
                sbuf[b, j, q] = tiles[b]
                low[b], high[b] = pack_edges(m, low[b], high[b], lane_roll(tiles[b], 2 * q), q)
        for b in range(4):
            sbuf[(b + 1) % 4, j, TILES] = lane_roll(high[b], -32)
            sbuf[(b + 3) % 4, j, TILES + 1] = lane_roll(low[b], 32)

    def met_copy(k):
        return remote(ms.at[group(k)], mr.at[t], met_s.at[k - 1], met_r.at[k - 1], (group(k), s))

    def met_arrival(k):
        return remote(ms.at[t], mr.at[group(4 - k)], met_s.at[k - 1], met_r.at[k - 1], (group(k), s))

    def xin_copy(k, j):
        return remote(
            sbuf.at[group(k), j], region.at[t * PER + j],
            xin_s.at[k - 1, j], xin_r.at[k - 1, j], (group(k), s),
        )

    def xin_arrival(k, j):
        return remote(
            sbuf.at[t, j], region.at[group(4 - k) * PER + j],
            xin_s.at[k - 1, j], xin_r.at[k - 1, j], (group(k), s),
        )

    def forward(src, i):
        return (
            remote(src, hl0.at[i], fw_s.at[0, i], fw_r.at[0, i], right),
            remote(src, hr0.at[i], fw_s.at[1, i], fw_r.at[1, i], left),
        )

    def own_copy(j):
        return pltpu.make_async_copy(sbuf.at[t, j], region.at[t * PER + j], own_sem.at[j])

    mr[t] = ms[t]
    pl.semaphore_wait(barrier, 5)
    for k in (2, 1, 3):
        met_copy(k).start()

    @pl.loop(0, PER)
    def _(j):
        pack(j)

        @pl.when(upper)
        def _():
            for k in (2, 1, 3):
                xin_copy(k, j).start()

        for c in forward(sbuf.at[t, j, pl.ds(0, TILES)], t * PER + j):
            c.start()
        own_copy(j).start()

    @pl.when(upper)
    def _():
        pl.semaphore_signal(go, inc=1, device_id=left, device_id_type=MESH)

    @pl.when(jnp.logical_not(upper))
    def _():
        pl.semaphore_wait(go, 1)
        for j in range(PER):
            for k in (2, 1, 3):
                xin_copy(k, j).start()

    for k in (2, 1, 3):
        met_arrival(k).wait_recv()
    for quad in range(8):
        for e, tile in enumerate(swap_segments(m, [mr[b, quad] for b in range(4)])):
            mt[4 * quad + e] = tile
    plane_metrics = (
        remote(mt.at[pl.ds(16, 4)], mleft, pm_s.at[0], pm_r.at[0], right),
        remote(mt.at[pl.ds(3, 1)], mright, pm_s.at[1], pm_r.at[1], left),
    )
    for c in plane_metrics:
        c.start()
    for p in range(2):
        o = 16 * p
        vol = mt[o + 3]
        sy = [mt[o + 4 + c] for c in range(3)]
        geo_y = geometry(sy, vol, y_up(m, vol, lane_roll(vol, -32), 1))
        geo_z = geometry_known([mt[o + 7 + c] for c in range(3)], mt[o + 13])
        geo_l = geometry_known([mt[o + 10 + c] for c in range(3)], mt[o + 14])
        for c in range(5):
            gy[p, c] = geo_y[c]
            gz[p, 0, c] = geo_z[c]
            gz[p, 1, c] = geo_l[c]

    def cross(i, w_of, moved_of, low_pack, high_pack, first):
        for p in range(2):
            w = [w_of(f, p) for f in range(6)]
            prim = primitives(w)

            up = [y_up(m, w[f], lane_roll(w[f], -32), 1) for f in range(6)]
            flux, rad, sc = face(
                w, up,
                lambda f: y_up(m, w[f], lane_roll(w[f], -32), 2) - y_down(m, w[f], 1),
                prim, primitives(up), [gy[p, c] for c in range(5)], None if first else ry[i, p],
            )
            total = [flux[f] - y_down(m, flux[f], 1) for f in range(6)]
            total[5] = total[5] + mt[16 * p + 15] * w[5] * w[5] / w[0]
            if first:
                ry[i, p] = sc
                radii = rad + y_down(m, rad, 1) + 8.0 * mt[16 * p + 3]

            moved = [moved_of(f, p) for f in range(6)]
            at = [2 * f + p for f in range(6)]

            def shifted(f, mask, pack, k):
                return lane_roll(jnp.where(mask, pack, moved[f]), k - 2 * at[f])

            up = [shifted(f, m.zlo == 2 * at[f], high_pack, -1) for f in range(6)]
            down = [shifted(f, m.zlo == (2 * at[f] - 1) % 32, low_pack, 1) for f in range(6)]
            flux, rad, sc = face(
                w, up,
                lambda f: shifted(f, m.pair == at[f], high_pack, -2) - down[f],
                prim, primitives(up), [gz[p, 0, c] for c in range(5)], None if first else rz[i, p, 0],
            )
            total = [total[f] + flux[f] for f in range(6)]
            if first:
                rz[i, p, 0] = sc
                radii = radii + rad
            flux, rad, sc = face(
                down, w,
                lambda f: up[f] - shifted(f, m.pair == (at[f] - 1) % 16, low_pack, 2),
                primitives(down), prim, [gz[p, 1, c] for c in range(5)], None if first else rz[i, p, 1],
            )
            if first:
                rz[i, p, 1] = sc
                den[i, p] = radii + rad
            for f in range(6):
                res[i, 2 * f + p] = total[f] - flux[f]

    def mix(w_of, first):
        pc = [0.5 * (table_entry(d) + table_entry(d - 8)) for d in range(5)]
        qc = [0.5 * (table_entry(d) - table_entry(d - 8)) for d in range(5)]

        @pl.loop(0, TILES)
        def _(q):
            vol = mt[lax.rem(q, 2) * 16 + 3]
            w = [w_of(i, q) for i in range(NINST)]
            b = [w[i] + w[i + 8] for i in range(8)]
            a = [w[i] - w[i + 8] for i in range(8)]
            a = a + [-x for x in a]
            for r in range(8):
                even = None
                odd = qc[4] * a[(r - 4) % 16]
                for d in range(1, 4):
                    e = pc[d] * (b[(r - d) % 8] - b[(r + d) % 8])
                    even = e if even is None else even + e
                    odd = odd + qc[d] * (a[(r - d) % 16] - a[(r + d) % 16])
                for i, v in ((r, even + odd), (r + 8, even - odd)):
                    v = vol * v
                    if first:
                        res[i, q] = res[i, q] + v
                    else:
                        coupling[i, q] = v

    def axial(i, w_of, hl, hr, first):
        planes = [
            [hl[i, 2 * f] for f in range(6)],
            [hl[i, 2 * f + 1] for f in range(6)],
            [w_of(f, 0) for f in range(6)],
            [w_of(f, 1) for f in range(6)],
            [hr[i, 2 * f] for f in range(6)],
            [hr[i, 2 * f + 1] for f in range(6)],
        ]
        prims = [primitives(w) for w in planes[1:5]]
        fluxes, radii = [], []
        for k in range(3):
            geo = [gx[k, c] for c in range(5)]
            fx, rad, sc = face(
                planes[k + 1], planes[k + 2], lambda f, k=k: planes[k + 3][f] - planes[k][f],
                prims[k], prims[k + 1], geo, None if first else rx[i, k],
            )
            if first:
                rx[i, k] = sc
            fluxes.append(fx)
            radii.append(rad)
        if first:
            for p in range(2):
                step[i, p] = 0.5 / (den[i, p] + radii[p] + radii[p + 1])
        return [[fluxes[p + 1][f] - fluxes[p][f] for f in range(6)] for p in range(2)]

    def arrival_order(n):
        far = jnp.maximum(n - PER, 0)
        own = n < PER
        j = jnp.where(own, n, far // 3)
        back = jnp.where(own, 0, lax.rem(far, 3) + 1)
        return j, lax.rem(t + nt - back, nt) * PER + j

    def block_order(n):
        return n // 4, lax.rem(t + nt - lax.rem(n, 4), nt) * PER + n // 4

    def plane_copies(i):
        return (
            remote(w1.at[i], hl1.at[i], wp_s.at[0, i], wp_r.at[0, i], right),
            remote(w1.at[i], hr1.at[i], wp_s.at[1, i], wp_r.at[1, i], left),
        )

    def column_copies(i):
        return (
            remote(zs.at[i, 0], z1.at[i, 1], z_s.at[0, i], z_r.at[0, i], (group(3), s)),
            remote(zs.at[i, 1], z1.at[i, 0], z_s.at[1, i], z_r.at[1, i], (group(1), s)),
        )

    def receive_block(j):
        sources = [(k, lax.rem(t + nt - k, nt) * PER + j) for k in (1, 3, 2)]
        for k, i in sources:
            xin_arrival(k, j).wait_recv()
            for c in forward(region.at[i, pl.ds(0, TILES)], i):
                c.start()

    def face_metrics():
        for c in plane_metrics:
            c.wait_recv()
        sx = [[mleft[c] for c in range(3)], [mt[c] for c in range(3)], [mt[16 + c] for c in range(3)]]
        vx = [mleft[3], mt[3], mt[19], mright[0]]
        for k in range(3):
            for c, g in enumerate(geometry(sx[k], vx[k], vx[k + 1])):
                gx[k, c] = g

    def second_cross(i):
        for c in column_copies(i):
            c.wait_recv()
        cross(
            i,
            lambda f, p: w1[i, 2 * f + p],
            lambda f, p: moved1[i, 2 * f + p],
            z1[i, 0], z1[i, 1], False,
        )

    @pl.loop(0, 2 * NINST)
    def _(n):
        k = n - NINST

        @pl.when(n < NINST)
        def _():
            j, i = arrival_order(n)

            @pl.when(n < PER)
            def _():
                own_copy(j).wait()

            @pl.when((n >= PER) & (lax.rem(jnp.maximum(n - PER, 0), 3) == 0))
            def _():
                receive_block(j)

            cross(
                i,
                lambda f, p: region[i, 2 * f + p],
                lambda f, p: lane_roll(region[i, 2 * f + p], 2 * (2 * f + p)),
                region[i, TILES], region[i, TILES + 1], True,
            )

        @pl.when(n == LAG)
        def _():
            face_metrics()

        @pl.when(k == 0)
        def _():
            mix(lambda i, q: region[i, q], True)

        @pl.when(k >= AHEAD)
        def _():
            second_cross(block_order(jnp.maximum(k - AHEAD, 0))[1])

        late = (k >= PER) & (lax.rem(n, 4) != 0)

        @pl.when(((n >= LAG) & (n < NINST)) | late)
        def _():
            i = jnp.where(n < NINST, arrival_order(n - LAG)[1], block_order(jnp.maximum(k, 0))[1])
            for c in forward(region.at[i, pl.ds(0, TILES)], i):
                c.wait_recv()
            change = axial(i, lambda f, p: region[i, 2 * f + p], hl0, hr0, True)
            for p in range(2):
                for f in range(6):
                    res[i, 2 * f + p] = res[i, 2 * f + p] + change[p][f]

        @pl.when(k >= 0)
        def _():
            j, i = block_order(jnp.maximum(k, 0))
            low = high = None
            for q in range(TILES):
                v = region[i, q] - 0.5 * step[i, q % 2] * res[i, q]
                w1[i, q] = v
                moved = lane_roll(v, 2 * q)
                moved1[i, q] = moved
                low, high = pack_edges(m, low, high, moved, q)
            zs[i, 0] = lane_roll(low, 32)
            zs[i, 1] = lane_roll(high, -32)
            for c in plane_copies(i) + column_copies(i):
                c.start()

    mix(lambda i, q: w1[i, q], False)

    def out_copy(k, j):
        g = group(k)
        return remote(
            ob.at[g * PER + j], oin.at[t, j], o_s.at[k - 1, j], o_r.at[k - 1, j], (g, s)
        )

    def out_arrival(k, j):
        return remote(
            ob.at[t * PER + j], oin.at[group(4 - k), j],
            o_s.at[k - 1, j], o_r.at[k - 1, j], (group(k), s),
        )

    def store_out(j):
        return pltpu.make_async_copy(ov.at[j], out.at[j], out_sem.at[j])

    @pl.loop(0, NINST)
    def _(n):
        j, i = block_order(n)
        back = lax.rem(n, 4)

        @pl.when(n >= NINST - AHEAD)
        def _():
            second_cross(i)

        for c in plane_copies(i):
            c.wait_recv()
        change = axial(i, lambda f, p: w1[i, 2 * f + p], hl1, hr1, False)
        for p in range(2):
            for f in range(6):
                ob[i, 2 * f + p] = -step[i, p] * (res[i, 2 * f + p] + coupling[i, 2 * f + p] + change[p][f])

        @pl.when(back > 0)
        def _():
            out_copy(4 - back, j).start()

        @pl.when(back == 0)
        def _():
            for q in range(TILES):
                oin[t, j, q] = ob[i, q]

    for k in (1, 2, 3):
        met_copy(k).wait_send()
    for c in plane_metrics:
        c.wait_send()

    @pl.loop(0, PER)
    def _(j):
        for k in (1, 2, 3):
            xin_copy(k, j).wait_send()

    @pl.loop(0, NINST)
    def _(i):
        for c in forward(region.at[i, pl.ds(0, TILES)], i):
            c.wait_send()
        for c in plane_copies(i) + column_copies(i):
            c.wait_send()

    @pl.loop(0, PER)
    def _(j):
        for k in range(1, 4):
            out_arrival(k, j).wait_recv()
        for q in range(TILES):
            f, p = divmod(q, 2)
            tiles = swap_segments(m, [oin[b, j, q] for b in range(4)])
            for y in range(4):
                ov[j, f, p, 8 * y : 8 * y + 8, :] = tiles[y]
        store_out(j).start()

    @pl.loop(0, PER)
    def _(j):
        for k in (1, 2, 3):
            out_copy(k, j).wait_send()

    for j in range(PER):
        store_out(j).wait()


def per_device(flow_state, metrics):
    tile = (8, 128)
    f32 = jnp.float32

    def vmem(*lead):
        return pltpu.VMEM(lead + tile, f32)

    dma = pltpu.SemaphoreType.DMA
    full = (NINST, TILES)
    return pl.pallas_call(
        kernel,
        out_shape=jax.ShapeDtypeStruct(flow_state.shape, f32),
        in_specs=[pl.BlockSpec(memory_space=pl.ANY)] * 2,
        out_specs=pl.BlockSpec(memory_space=pl.ANY),
        scratch_shapes=[
            pltpu.VMEM(flow_state.shape, f32),
            pltpu.VMEM(metrics.shape, f32),
            vmem(GROUPS, PER, TILES + 2),
            vmem(NINST, TILES + 2),
            vmem(*full),
            vmem(*full),
            vmem(*full),
            vmem(*full),
            vmem(*full),
            vmem(*full),
            vmem(NINST, 2),
            vmem(NINST, 2),
            vmem(*full),
            vmem(*full),
            vmem(*full),
            vmem(GROUPS, PER, TILES),
            pltpu.VMEM(flow_state.shape, f32),
            vmem(4, 8),
            vmem(4, 8),
            vmem(32),
            vmem(4),
            vmem(1),
            vmem(3, 5),
            vmem(2, 5),
            vmem(2, 2, 5),
            vmem(NINST, 2),
            vmem(NINST, 2, 2),
            vmem(NINST, 3),
            vmem(NINST, 2),
            vmem(NINST, 2),
            dma((PER + 1,)),
            dma((PER,)),
            dma((PER,)),
            dma((3,)),
            dma((3,)),
            dma((2,)),
            dma((2,)),
            pltpu.SemaphoreType.REGULAR,
            dma((3, PER)),
            dma((3, PER)),
            dma((2, NINST)),
            dma((2, NINST)),
            dma((2, NINST)),
            dma((2, NINST)),
            dma((2, NINST)),
            dma((2, NINST)),
            dma((3, PER)),
            dma((3, PER)),
        ],
        compiler_params=pltpu.CompilerParams(
            collective_id=0, has_side_effects=True, vmem_limit_bytes=53 << 20
        ),
        cost_estimate=pl.CostEstimate(
            flops=100_000_000, bytes_accessed=1_800_000, transcendentals=200_000
        ),
        name="balance",
    )(flow_state, metrics)


def solution(mesh):
    return jax.shard_map(
        per_device,
        mesh=mesh,
        in_specs=(P("tm", None, "space", None, None), P(None, "space", "tm", None)),
        out_specs=P("tm", None, "space", None, None),
        check_vma=False,
    )
```
